512 devices in a mesh: mem: 16 (over z, core), reg: 32 (over y, x).
Axes of the slice: x: 4, y: 8, z: 8, core: 2. Of those that a mesh axis runs over, the one named last changes fastest.
Arguments:
- starting_sample_set: float32 [80, 4, 128, 1024], P('mem', None, 'reg'), may hold values from -6 to 6
- block_owner: int32 [3], replicated, may hold values from 0 to 31, as said below
- obs_location: int32 [3, 512], replicated, may hold values from 0 to 16383
- taper_pairs: int32 [3, 2], replicated, may hold values from 64 to 256, as said below
- obs_values: float32 [3, 512], replicated, may hold values from -6 to 6
- obs_noise: float32 [3, 80, 512], replicated, may hold values from -5 to 5
- obs_variance: float32 [3, 512], replicated, may hold values from 0.2 to 2
Outputs:
- analysis: float32 [80, 524288], P(None, ('reg', 'mem'))
The draws below stay inside these ranges and needn't reach their ends.
Inputs may be any that keep to these rules, and one draw needn't show every extreme that they name: `block_owner`: the owners of the blocks are distinct regions. `taper_pairs`: column 0 is a row half-width from 64 to 128 and column 1 a column half-width from 64 to 256; each of these four ends is taken by some block in every draw.
All inputs are finite; a program needn't handle non-finite values.
Results may differ from the reference program's by a relative error of at most 0.00019.
Values sent between devices are 32-bit elements; how exact they have to be, the bound alone decides.
No kernel may reach another device: no remote copies, remote signals or barrier semaphores. Data moves between devices by JAX's collectives and lax.ppermute only.
A program may use at most 64 MiB of HBM per device.

```python
import math
import jax
import jax.numpy as jnp
from jax import lax

SUBDOMAIN_LINES = 4
NY = 1024
FIELDS = 4
STEPS = 4
OBS = 512
BLOCKS = 3
MEMBERS = 80
NX = 128
VARS_REG = 16384
N_REG = 32


def draw_block_owner(key, part):
    key = jax.random.fold_in(key, 7)
    key_mid, key_order = jax.random.split(key, 2)
    middle = 1 + jax.random.permutation(key_mid, N_REG - 2)
    ends = jnp.array([0, N_REG - 1], dtype=jnp.int32)
    chosen = jnp.concatenate([ends, middle.astype(jnp.int32)])[:BLOCKS]
    ordering = jax.random.permutation(key_order, BLOCKS)
    return chosen[ordering].astype(jnp.int32)


def draw_taper_pairs(key, part):
    key = jax.random.fold_in(key, 11)
    key_row, key_col, key_pick = jax.random.split(key, 3)
    grid_rows = SUBDOMAIN_LINES * N_REG
    row_width = jax.random.randint(key_row, (BLOCKS,), grid_rows // 2, grid_rows + 1)
    col_width = jax.random.randint(key_col, (BLOCKS,), NY // 16, NY // 4 + 1)
    ordering = jax.random.permutation(key_pick, BLOCKS)
    narrow = ordering[0]
    widest = ordering[1]
    indices = jnp.arange(BLOCKS)
    row_width = jnp.where(indices == narrow, grid_rows // 2, jnp.where(indices == widest, grid_rows, row_width))
    col_width = jnp.where(indices == narrow, NY // 16, jnp.where(indices == widest, NY // 4, col_width))
    return jnp.stack([row_width, col_width], axis=1).astype(jnp.int32)


def touch_ends(values, stream_key, least, top_value):
    dims = values.shape
    place = [jax.random.randint(jax.random.fold_in(stream_key, axis), (), 0, dims[axis]) for axis in range(len(dims))]
    values = values.at[tuple(place)].set(least)
    longest = dims.index(max(dims))
    place[longest] = (place[longest] + 1) % dims[longest]
    return values.at[tuple(place)].set(top_value)


def block_scale(key, shape, cuts, smallest, high):
    level = 1.0
    for dim, shards_of in cuts:
        steps = jax.random.uniform(jax.random.fold_in(jax.random.fold_in(key, 6), dim), (shards_of,), jnp.float32, smallest / len(cuts), high / len(cuts))
        level = level * jnp.repeat(jnp.exp(steps), shape[dim] // shards_of).reshape((-1,) + (1,) * (len(shape) - 1 - dim))
    return level


def gaussian(own_key, extent, scale, limit, cuts=(), kind=jnp.bfloat16):
    factor_of = block_scale(own_key, extent, cuts, -0.22, 0.18) if cuts else 1.0
    drawn = jax.random.normal(own_key, extent, jnp.float32) * scale * factor_of
    return jnp.minimum(jnp.maximum(drawn, -limit), limit).astype(kind)


def setup_inputs(seed: int = 0) -> dict:
    key_of = jax.random.split(jax.random.key(seed), 8)
    starting_sample_set = gaussian(key_of[0], (MEMBERS, FIELDS, NX, NY), 1.0, 6.0, ((0, 16), (2, 32)), jnp.float32)
    block_owner = draw_block_owner(jax.random.fold_in(key_of[7], 71), 0)
    obs_location = touch_ends(jax.random.randint(key_of[2], (BLOCKS, OBS), 0, VARS_REG), jax.random.fold_in(key_of[2], 1), 0, VARS_REG - 1).astype(jnp.int32)
    taper_pairs = draw_taper_pairs(jax.random.fold_in(key_of[7], 71), 0)
    obs_values = gaussian(key_of[4], (BLOCKS, OBS), 1.0, 6.0, (), jnp.float32)
    obs_noise = gaussian(key_of[5], (BLOCKS, MEMBERS, OBS), 0.7, 5.0, (), jnp.float32)
    obs_variance = jnp.clip(jnp.exp(jax.random.uniform(key_of[6], (BLOCKS, OBS), jnp.float32, math.log(0.2), math.log(2.0))), 0.2, 2.0)
    return dict(starting_sample_set=starting_sample_set, block_owner=block_owner, obs_location=obs_location, taper_pairs=taper_pairs, obs_values=obs_values, obs_noise=obs_noise, obs_variance=obs_variance)


mixing = 0.1
courant = 0.05
gravity = 1.0
rotation = 0.02
highest = lax.Precision.HIGHEST

def advance(center, row_above, row_below, col_west, col_east):
    smooth = (1.0 - mixing) * center + mixing * 0.25 * (row_above + row_below + col_west + col_east)
    col_diff = col_east - col_west
    row_diff = row_below - row_above
    speed_u = center[:, 1:2]
    speed_v = center[:, 2:3]
    carried = speed_u * col_diff + speed_v * row_diff
    net_flux = (1.0 + col_east[:, 0]) * col_east[:, 1] - (1.0 + col_west[:, 0]) * col_west[:, 1] + (1.0 + row_below[:, 0]) * row_below[:, 2] - (1.0 + row_above[:, 0]) * row_above[:, 2]
    new_depth = smooth[:, 0] - courant * net_flux
    new_east = smooth[:, 1] - courant * (carried[:, 1] + gravity * col_diff[:, 0]) + rotation * center[:, 2]
    new_north = smooth[:, 2] - courant * (carried[:, 2] + gravity * row_diff[:, 0]) - rotation * center[:, 1]
    new_tracer = smooth[:, 3] - courant * carried[:, 3]
    return jnp.stack([new_depth, new_east, new_north, new_tracer], axis=1)

def taper_weight(row_first, col_first, row_second, col_second, widths, meridional_extent, lateral_extent):
    gap_row = jnp.abs(row_first[:, None] - row_second[None, :])
    gap_row = jnp.minimum(gap_row, meridional_extent - gap_row)
    gap_col = jnp.abs(col_first[:, None] - col_second[None, :])
    gap_col = jnp.minimum(gap_col, lateral_extent - gap_col)
    weight_row = jnp.maximum(0.0, 1.0 - gap_row.astype(jnp.float32) / widths[0].astype(jnp.float32))
    weight_col = jnp.maximum(0.0, 1.0 - gap_col.astype(jnp.float32) / widths[1].astype(jnp.float32))
    return weight_row * weight_col

def gain_weights(predicted, obs_row, obs_col, widths, variance, values, noise, meridional_extent, lateral_extent):
    realization_array = predicted.shape[0]
    obs_anomaly = predicted - jnp.mean(predicted, axis=0, keepdims=True)
    spread = lax.dot_general(obs_anomaly, obs_anomaly, (((0,), (0,)), ((), ())), precision=highest) / (realization_array - 1)
    innovation_cov = taper_weight(obs_row, obs_col, obs_row, obs_col, widths, meridional_extent, lateral_extent) * spread + jnp.diag(variance)
    factor = jnp.linalg.cholesky(innovation_cov)
    misfit = values[None, :] + noise - predicted
    weights = jax.scipy.linalg.cho_solve((factor, True), misfit.T).T
    return (obs_anomaly, weights)

def assimilate(state_rows, var_row, var_col, obs_anomaly, weights, obs_row, obs_col, widths, meridional_extent, lateral_extent):
    realization_array = state_rows.shape[0]
    centered = state_rows - jnp.mean(state_rows, axis=0, keepdims=True)
    cross_cov = lax.dot_general(centered, obs_anomaly, (((0,), (0,)), ((), ())), precision=highest) / (realization_array - 1)
    tapered = taper_weight(var_row, var_col, obs_row, obs_col, widths, meridional_extent, lateral_extent) * cross_cov
    return state_rows + lax.dot_general(weights, tapered, (((1,), (1,)), ((), ())), precision=highest)

def propagate_single_realization(realization_quantities):
    fields_now = realization_quantities[None]
    for counter in range(STEPS):
        fields_now = advance(fields_now, jnp.roll(fields_now, 1, axis=2), jnp.roll(fields_now, -1, axis=2), jnp.roll(fields_now, 1, axis=3), jnp.roll(fields_now, -1, axis=3))
    return fields_now[0]

def reference(starting_sample_set, block_owner, obs_location, taper_pairs, obs_values, obs_noise, obs_variance):
    propagated_quantities = lax.map(propagate_single_realization, starting_sample_set)
    realization_array, gridded_quantity_array, meridional_extent, lateral_extent = propagated_quantities.shape
    subdomain_sequence = meridional_extent // SUBDOMAIN_LINES
    current_model_vector = propagated_quantities.reshape(realization_array, gridded_quantity_array, subdomain_sequence, SUBDOMAIN_LINES, lateral_extent)
    current_model_vector = current_model_vector.transpose(2, 0, 1, 3, 4).reshape(subdomain_sequence, realization_array, VARS_REG)
    var_index = jnp.arange(VARS_REG, dtype=jnp.int32)
    region_ids = jnp.arange(subdomain_sequence, dtype=jnp.int32)
    for block_id in range(BLOCKS):
        owner_reg = block_owner[block_id]
        obs_cell = obs_location[block_id]
        widths = taper_pairs[block_id]
        owner_state = lax.dynamic_index_in_dim(current_model_vector, owner_reg, 0, keepdims=False)
        predicted = jnp.take(owner_state, obs_cell, axis=1)
        obs_row = owner_reg * SUBDOMAIN_LINES + obs_cell // lateral_extent % SUBDOMAIN_LINES
        obs_col = obs_cell % lateral_extent
        obs_anomaly, weights = gain_weights(predicted, obs_row, obs_col, widths, obs_variance[block_id], obs_values[block_id], obs_noise[block_id], meridional_extent, lateral_extent)

        def update_region(region_pair):
            state_rows, region = region_pair
            var_row = region * SUBDOMAIN_LINES + var_index // lateral_extent % SUBDOMAIN_LINES
            var_col = var_index % lateral_extent
            return assimilate(state_rows, var_row, var_col, obs_anomaly, weights, obs_row, obs_col, widths, meridional_extent, lateral_extent)
        current_model_vector = lax.map(update_region, (current_model_vector, region_ids))
    return current_model_vector.transpose(1, 0, 2).reshape(realization_array, subdomain_sequence * VARS_REG)
```

```python
import jax
import jax.numpy as jnp
from jax import lax
from jax.experimental import pallas as pl
from jax.experimental.pallas import tpu as pltpu
from jax.sharding import PartitionSpec as P

STEPS = 4
MIX = 0.1
COURANT = 0.05
ROTATION = 0.02
LANES = 128
GROUP = 8
highest = lax.Precision.HIGHEST
f32 = jnp.float32
bf16 = jnp.bfloat16

vmem = pl.BlockSpec(memory_space=pltpu.VMEM)
smem = pl.BlockSpec(memory_space=pltpu.SMEM)
params = pltpu.CompilerParams(vmem_limit_bytes=48 * 1024 * 1024)


def dot_exact(a, b):
    return lax.dot_general(
        a, b, (((1,), (0,)), ((), ())), precision=highest, preferred_element_type=f32
    )


def dot_bf16(a, b):
    return lax.dot_general(a, b, (((1,), (0,)), ((), ())), preferred_element_type=f32)


def halves(x):
    hi = x.astype(bf16)
    return hi, (x - hi.astype(f32)).astype(bf16)


def thirds(x):
    hi = x.astype(bf16)
    rest = x - hi.astype(f32)
    mid = rest.astype(bf16)
    return hi, mid, (rest - mid.astype(f32)).astype(bf16)


def dot_split(a, b):
    a_hi, a_lo = halves(a)
    b_hi, b_lo = halves(b)
    return dot_bf16(
        jnp.concatenate([a_hi, a_hi, a_lo], axis=1), jnp.concatenate([b_hi, b_lo, b_hi], axis=0)
    )


def tree_sum(terms):
    terms = list(terms)
    while len(terms) > 1:
        terms = [
            terms[i] + terms[i + 1] if i + 1 < len(terms) else terms[i]
            for i in range(0, len(terms), 2)
        ]
    return terms[0]


def forecast_kernel(above, own, below, loc, state_out, picked_out, rows, columns):
    members, fields, lines, width = own.shape
    pad = rows.shape[2]
    n_rows = fields * lines * GROUP
    rows[:, :, 0:lines, :] = above[...]
    rows[:, :, lines : 2 * lines, :] = own[...]
    rows[:, :, 2 * lines : 3 * lines, :] = below[...]
    rows[:, :, 3 * lines : pad, :] = jnp.zeros((members, fields, pad - 3 * lines, width), f32)
    columns[...] = jnp.zeros(columns.shape, f32)

    def member(m, carry):
        c = [rows[m, f] for f in range(fields)]
        for _ in range(STEPS):
            n = [pltpu.roll(x, 1, 0) for x in c]
            s = [pltpu.roll(x, pad - 1, 0) for x in c]
            w = [pltpu.roll(x, 1, 1) for x in c]
            e = [pltpu.roll(x, width - 1, 1) for x in c]
            smooth = [
                (1.0 - MIX) * c[f] + MIX * 0.25 * (n[f] + s[f] + w[f] + e[f]) for f in range(fields)
            ]
            dc = [e[f] - w[f] for f in range(fields)]
            dr = [s[f] - n[f] for f in range(fields)]
            carried = [c[1] * dc[f] + c[2] * dr[f] for f in range(fields)]
            flux = (
                (1.0 + e[0]) * e[1]
                - (1.0 + w[0]) * w[1]
                + (1.0 + s[0]) * s[2]
                - (1.0 + n[0]) * n[2]
            )
            c = [
                smooth[0] - COURANT * flux,
                smooth[1] - COURANT * (carried[1] + dc[0]) + ROTATION * c[2],
                smooth[2] - COURANT * (carried[2] + dr[0]) - ROTATION * c[1],
                smooth[3] - COURANT * carried[3],
            ]
        for f in range(fields):
            mine = c[f][lines : 2 * lines]
            for t in range(width // LANES):
                at = t * n_rows + f * lines * GROUP + m
                columns[pl.ds(at, lines, stride=GROUP), :] = mine[:, t * LANES : (t + 1) * LANES]
                at = f * lines * members * GROUP + m * GROUP + t
                state_out[pl.ds(at, lines, stride=members * GROUP), :] = mine[
                    :, t * LANES : (t + 1) * LANES
                ]
        return carry

    lax.fori_loop(0, members, member, 0)

    where = loc[...]
    count = where.shape[1]
    column = where % width
    line = where // width
    onehot = (lax.broadcasted_iota(jnp.int32, (width, count), 0) == column).astype(f32).astype(bf16)
    parts = thirds(
        jnp.concatenate(
            [columns[t * n_rows : (t + 1) * n_rows, :] for t in range(width // LANES)], axis=1
        )
    )
    taken = dot_bf16(jnp.concatenate(parts, axis=0), onehot)
    taken = taken[:n_rows] + taken[n_rows : 2 * n_rows] + taken[2 * n_rows :]
    picked = tree_sum(
        jnp.where(line == d, taken[d * GROUP : (d + 1) * GROUP], 0.0)
        for d in range(fields * lines)
    )[:members]
    for r in range(picked_out.shape[0]):
        picked_out[r] = picked


def forecast(above, own, below, loc, regions):
    members, fields, lines, width = own.shape
    assert width == GROUP * LANES and members <= GROUP
    n_dest = fields * lines
    return pl.pallas_call(
        forecast_kernel,
        out_shape=[
            jax.ShapeDtypeStruct((n_dest * members * GROUP, LANES), f32),
            jax.ShapeDtypeStruct((regions, members, loc.shape[1]), f32),
        ],
        in_specs=[vmem] * 4,
        out_specs=[vmem] * 2,
        scratch_shapes=[
            pltpu.VMEM((members, fields, 4 * lines, width), f32),
            pltpu.VMEM((n_dest * GROUP * GROUP, LANES), f32),
        ],
        compiler_params=params,
        name="forecast",
    )(above, own, below, loc)


def lane_bcast(x, j):
    return jnp.broadcast_to(x[:, j : j + 1], x.shape)


def row_bcast(x, j):
    return jnp.broadcast_to(x[j : j + 1, :], x.shape)


def eliminate(m, p):
    lane = lax.broadcasted_iota(jnp.int32, (GROUP, LANES), 1)
    sub = lax.broadcasted_iota(jnp.int32, (GROUP, LANES), 0)
    base = GROUP * p
    here = (lane >= base) & (lane < base + GROUP)
    panel = m[p]
    col = [lane_bcast(panel, base + j) for j in range(GROUP)]
    panel = jnp.where(here, (lane - base == sub).astype(f32), panel)
    for j in range(GROUP):
        inv = pltpu.reciprocal(row_bcast(col[j], j))
        mine = sub == j
        row = row_bcast(panel, j) * inv
        panel = jnp.where(mine, row, panel - col[j] * row)
        for i in range(j + 1, GROUP):
            row = row_bcast(col[i], j) * inv
            col[i] = jnp.where(mine, row, col[i] - col[j] * row)
    bcast = [row_bcast(panel, j) for j in range(GROUP)]
    n = len(m)
    out = list(m)
    out[p] = panel
    for t in range(1, n):
        g = (p + t) % n
        out[g] = jnp.where(here, 0.0, m[g]) - tree_sum(
            lane_bcast(m[g], base + j) * bcast[j] for j in range(GROUP)
        )
    return out


def inverse_128(block):
    m = [block[GROUP * g : GROUP * (g + 1), :] for g in range(LANES // GROUP)]
    for p in range(LANES // GROUP):
        m = eliminate(m, p)
    return jnp.concatenate(m, axis=0)


def ring_taper(first, second, extent, inv_width):
    gap = jnp.abs(first - second)
    gap = jnp.minimum(gap, extent - gap)
    return jnp.maximum(0.0, 1.0 - gap * inv_width)


def down(row, n):
    return jnp.broadcast_to(row, (LANES, n)).T


def solve_kernel(
    inv_width, gathered, place, values, noise, variance, anom_out, weight_out, pred, cov, rhs, *, extents
):
    rows_all, cols_all = extents
    senders, blocks, per, count = gathered.shape
    members = senders * per
    tiles = count // LANES
    scale = 1.0 / (members - 1)
    for b in range(blocks):
        for s in range(senders):
            pred[b, s * per : (s + 1) * per, :] = gathered[s, b]

    def taper(b, c):
        row_b = down(place[b, 0:1, :], count)
        col_b = down(place[b, 1:2, :], count)
        row_c = place[c, 0:1, :]
        col_c = place[c, 1:2, :]
        return jnp.concatenate(
            [
                ring_taper(row_b, row_c[:, t * LANES : (t + 1) * LANES], rows_all, inv_width[b, 0])
                * ring_taper(col_b, col_c[:, t * LANES : (t + 1) * LANES], cols_all, inv_width[b, 1])
                for t in range(tiles)
            ],
            axis=1,
        )

    def block(b, carry):
        now = pred[b]
        anom = now - jnp.sum(now, axis=0, keepdims=True) * (1.0 / members)
        anom_out[b] = anom
        anom_t = anom.T
        spread = dot_exact(anom_t, anom) * scale
        diag = lax.broadcasted_iota(jnp.int32, (count, count), 0) == lax.broadcasted_iota(
            jnp.int32, (count, count), 1
        )
        cov[...] = taper(b, b) * spread + jnp.where(diag, variance[b], 0.0)
        rhs[...] = values[b] + noise[b] - now
        for k in range(tiles):
            at = slice(k * LANES, (k + 1) * LANES)
            after = slice((k + 1) * LANES, count)
            inv = inverse_128(cov[at, at])
            top = dot_exact(rhs[:, at], inv)
            rhs[:, at] = top
            if k + 1 < tiles:
                low = dot_exact(cov[after, at], inv)
                cov[after, at] = low
                across = cov[at, after]
                rhs[:, after] -= dot_exact(top, across)
                cov[after, after] -= dot_exact(low, across)
        for k in reversed(range(tiles - 1)):
            at = slice(k * LANES, (k + 1) * LANES)
            after = slice((k + 1) * LANES, count)
            rhs[:, at] -= dot_exact(rhs[:, after], cov[after, at])
        weight = rhs[...]
        weight_out[b] = weight

        def later(c, carry):
            now = pred[c]
            anom_c = now - jnp.sum(now, axis=0, keepdims=True) * (1.0 / members)
            cross = taper(b, c) * (dot_exact(anom_t, anom_c) * scale)
            pred[c] = now + dot_exact(weight, cross)
            return carry

        lax.fori_loop(b + 1, blocks, later, 0)
        return carry

    lax.fori_loop(0, blocks, block, 0)


def solve(inv_width, gathered, place, values, noise, variance, extents):
    senders, blocks, per, count = gathered.shape
    members = senders * per
    out = jax.ShapeDtypeStruct((blocks, members, count), f32)

    def body(*refs):
        solve_kernel(*refs, extents=extents)

    return pl.pallas_call(
        body,
        out_shape=[out, out],
        in_specs=[smem] + [vmem] * 5,
        out_specs=[vmem, vmem],
        scratch_shapes=[
            pltpu.VMEM((blocks, members, count), f32),
            pltpu.VMEM((count, count), f32),
            pltpu.VMEM((members, count), f32),
        ],
        compiler_params=params,
        name="solve",
    )(inv_width, gathered, place, values[:, None, :], noise, variance[:, None, :])


def update_kernel(inv_width, my_row, state, place, anom, weight, out, *, extents):
    rows_all, cols_all = extents
    blocks, members, count = anom.shape
    tiles = state.shape[0] // members
    for t in range(tiles):
        out[:, t * LANES : (t + 1) * LANES] = state[pl.ds(t, members, stride=tiles), :]
    row = my_row[0]
    for b in range(blocks):
        now = out[...]
        centered = now - jnp.sum(now, axis=0, keepdims=True) * (1.0 / members)
        cross = dot_split(anom[b].T, centered)
        obs_col = down(place[b, 1:2, :], count)
        lane = lax.broadcasted_iota(jnp.int32, (1, LANES), 1).astype(f32)
        by_row = ring_taper(row, place[b, 0:1, :], rows_all, inv_width[b, 0])
        by_col = jnp.concatenate(
            [
                ring_taper(obs_col, lane + float(t * LANES), cols_all, inv_width[b, 1])
                for t in range(tiles)
            ],
            axis=1,
        )
        out[...] = now + dot_split(weight[b] * (by_row * (1.0 / (members - 1))), by_col * cross)


def update(inv_width, my_row, state, place, anom, weight, extents):
    blocks, members, count = anom.shape
    tiles = state.shape[0] // members

    def body(*refs):
        update_kernel(*refs, extents=extents)

    return pl.pallas_call(
        body,
        out_shape=jax.ShapeDtypeStruct((members, tiles * LANES), f32),
        in_specs=[smem, smem] + [vmem] * 4,
        out_specs=vmem,
        compiler_params=params,
        name="update",
    )(inv_width, my_row, state, place, anom, weight)


def shards(
    starting_sample_set, block_owner, obs_location, taper_pairs, obs_values, obs_noise, obs_variance
):
    members, fields, lines, width = starting_sample_set.shape
    regions = lax.axis_size("reg")
    senders = lax.axis_size("mem")
    region = lax.axis_index("reg")
    mem_index = lax.axis_index("mem")
    extents = (float(lines * regions), float(width))
    assert fields * lines == senders

    forth = [(i, (i + 1) % regions) for i in range(regions)]
    back = [((i + 1) % regions, i) for i in range(regions)]
    above = lax.ppermute(starting_sample_set, "reg", forth)
    below = lax.ppermute(starting_sample_set, "reg", back)

    mine = jnp.argmax((block_owner == region).astype(jnp.int32))
    loc = lax.dynamic_slice_in_dim(obs_location, mine, 1, axis=0)
    state, picked = forecast(above, starting_sample_set, below, loc, regions)

    picked = lax.all_to_all(picked, "reg", 0, 0, tiled=True)
    picked = jnp.concatenate(
        [
            lax.dynamic_slice_in_dim(picked, block_owner[b], 1, axis=0)
            for b in range(obs_location.shape[0])
        ],
        axis=0,
    )
    gathered = lax.all_gather(picked, "mem")

    state = lax.all_to_all(
        state.reshape(senders, members * GROUP, LANES), "mem", 0, 0, tiled=True
    ).reshape(senders * members * GROUP, LANES)

    obs_row = block_owner[:, None] * lines + obs_location // width % lines
    obs_col = obs_location % width
    place = jnp.stack([obs_row, obs_col], axis=1).astype(f32)
    inv_width = 1.0 / taper_pairs.astype(f32)
    anom, weight = solve(inv_width, gathered, place, obs_values, obs_noise, obs_variance, extents)
    my_row = (region * lines + mem_index % lines).astype(f32).reshape(1)
    return update(inv_width, my_row, state, place, anom, weight, extents)


def solution(mesh):
    return jax.shard_map(
        shards,
        mesh=mesh,
        in_specs=(P("mem", None, "reg", None), P(), P(), P(), P(), P(), P()),
        out_specs=P(None, ("reg", "mem")),
        check_vma=False,
    )
```

```python
import jax
import jax.numpy as jnp
from jax import lax
from jax.experimental import pallas as pl
from jax.experimental.pallas import tpu as pltpu
from jax.sharding import PartitionSpec as P

STEPS = 4
MIX = 0.1
COURANT = 0.05
ROTATION = 0.02
LANES = 128
GROUP = 8
PANEL = 2
highest = lax.Precision.HIGHEST
f32 = jnp.float32
bf16 = jnp.bfloat16

vmem = pl.BlockSpec(memory_space=pltpu.VMEM)
smem = pl.BlockSpec(memory_space=pltpu.SMEM)
params = pltpu.CompilerParams(vmem_limit_bytes=48 * 1024 * 1024)


def dot_exact(a, b):
    return lax.dot_general(
        a, b, (((1,), (0,)), ((), ())), precision=highest, preferred_element_type=f32
    )


def dot_bf16(a, b):
    return lax.dot_general(a, b, (((1,), (0,)), ((), ())), preferred_element_type=f32)


def halves(x):
    hi = x.astype(bf16)
    return hi, (x - hi.astype(f32)).astype(bf16)


def thirds(x):
    hi = x.astype(bf16)
    rest = x - hi.astype(f32)
    mid = rest.astype(bf16)
    return hi, mid, (rest - mid.astype(f32)).astype(bf16)


def dot_split(a, b):
    a_hi, a_lo = halves(a)
    b_hi, b_lo = halves(b)
    return dot_bf16(
        jnp.concatenate([a_hi, a_hi, a_lo], axis=1), jnp.concatenate([b_hi, b_lo, b_hi], axis=0)
    )


def stacked(x):
    hi = x.astype(bf16).astype(f32)
    lo = x - hi
    return jnp.concatenate([hi, hi, lo], axis=0)


def dot_stacked(left, b):
    b_hi, b_lo = halves(b)
    return dot_bf16(left, jnp.concatenate([b_hi, b_lo, b_hi], axis=0))


def tree_sum(terms):
    terms = list(terms)
    while len(terms) > 1:
        terms = [
            terms[i] + terms[i + 1] if i + 1 < len(terms) else terms[i]
            for i in range(0, len(terms), 2)
        ]
    return terms[0]


def forecast_kernel(
    above, own, below, loc, state_out, picked_out, rows, columns, *, picked_rows
):
    members, fields, lines, width = own.shape
    pad = rows.shape[2]
    n_rows = fields * lines * GROUP
    rows[:, :, 0:lines, :] = above[...]
    rows[:, :, lines : 2 * lines, :] = own[...]
    rows[:, :, 2 * lines : 3 * lines, :] = below[...]
    rows[:, :, 3 * lines : pad, :] = jnp.zeros((members, fields, pad - 3 * lines, width), f32)
    columns[...] = jnp.zeros(columns.shape, f32)

    def member(m, carry):
        c = [rows[m, f] for f in range(fields)]
        for _ in range(STEPS):
            n = [pltpu.roll(x, 1, 0) for x in c]
            s = [pltpu.roll(x, pad - 1, 0) for x in c]
            w = [pltpu.roll(x, 1, 1) for x in c]
            e = [pltpu.roll(x, width - 1, 1) for x in c]
            smooth = [
                (1.0 - MIX) * c[f] + MIX * 0.25 * (n[f] + s[f] + w[f] + e[f]) for f in range(fields)
            ]
            dc = [e[f] - w[f] for f in range(fields)]
            dr = [s[f] - n[f] for f in range(fields)]
            carried = [c[1] * dc[f] + c[2] * dr[f] for f in range(fields)]
            flux = (
                (1.0 + e[0]) * e[1]
                - (1.0 + w[0]) * w[1]
                + (1.0 + s[0]) * s[2]
                - (1.0 + n[0]) * n[2]
            )
            c = [
                smooth[0] - COURANT * flux,
                smooth[1] - COURANT * (carried[1] + dc[0]) + ROTATION * c[2],
                smooth[2] - COURANT * (carried[2] + dr[0]) - ROTATION * c[1],
                smooth[3] - COURANT * carried[3],
            ]
        for f in range(fields):
            mine = c[f][lines : 2 * lines]
            for t in range(width // LANES):
                at = t * n_rows + f * lines * GROUP + m
                columns[pl.ds(at, lines, stride=GROUP), :] = mine[:, t * LANES : (t + 1) * LANES]
                at = f * lines * members * GROUP + m * GROUP + t
                state_out[pl.ds(at, lines, stride=members * GROUP), :] = mine[
                    :, t * LANES : (t + 1) * LANES
                ]
        return carry

    lax.fori_loop(0, members, member, 0)

    where = loc[...]
    count = where.shape[1]
    column = where % width
    line = where // width
    onehot = (lax.broadcasted_iota(jnp.int32, (width, count), 0) == column).astype(f32).astype(bf16)
    parts = thirds(
        jnp.concatenate(
            [columns[t * n_rows : (t + 1) * n_rows, :] for t in range(width // LANES)], axis=1
        )
    )
    taken = dot_bf16(jnp.concatenate(parts, axis=0), onehot)
    taken = taken[:n_rows] + taken[n_rows : 2 * n_rows] + taken[2 * n_rows :]
    picked = tree_sum(
        jnp.where(line == d, taken[d * GROUP : (d + 1) * GROUP], 0.0)
        for d in range(fields * lines)
    )[:members]
    chunks = count // LANES
    for r in range(picked_out.shape[0] // picked_rows):
        for t in range(chunks):
            picked_out[pl.ds(r * picked_rows + t, members, stride=chunks), :] = picked[
                :, t * LANES : (t + 1) * LANES
            ]


def forecast(above, own, below, loc, regions):
    members, fields, lines, width = own.shape
    assert width == GROUP * LANES and members <= GROUP
    n_dest = fields * lines
    picked_rows = -(-members * loc.shape[1] // (LANES * GROUP)) * GROUP

    def body(*refs):
        forecast_kernel(*refs, picked_rows=picked_rows)

    return pl.pallas_call(
        body,
        out_shape=[
            jax.ShapeDtypeStruct((n_dest * members * GROUP, LANES), f32),
            jax.ShapeDtypeStruct((regions * picked_rows, LANES), f32),
        ],
        in_specs=[vmem] * 4,
        out_specs=[vmem] * 2,
        scratch_shapes=[
            pltpu.VMEM((members, fields, 4 * lines, width), f32),
            pltpu.VMEM((n_dest * GROUP * GROUP, LANES), f32),
        ],
        compiler_params=params,
        name="forecast",
    )(above, own, below, loc)


def lane_bcast(x, j):
    return jnp.broadcast_to(x[:, j : j + 1], x.shape)


def row_bcast(x, j):
    return jnp.broadcast_to(x[j : j + 1, :], x.shape)


def eliminate(m, p, zeros):
    width = PANEL * GROUP
    lane = lax.broadcasted_iota(jnp.int32, (GROUP, LANES), 1)
    sub = lax.broadcasted_iota(jnp.int32, (GROUP, LANES), 0)
    base = width * p
    here = (lane >= base) & (lane < base + width)
    own = range(PANEL * p, PANEL * (p + 1))
    col = [[lane_bcast(m[g], base + j) + zeros for g in own] for j in range(width)]
    col.append(
        [
            jnp.where(here, (lane - base == sub + GROUP * i).astype(f32), m[g])
            for i, g in enumerate(own)
        ]
    )
    for j in range(width):
        mine, at = divmod(j, GROUP)
        inv = pltpu.reciprocal(row_bcast(col[j][mine], at))
        pivot = sub == at
        coef = list(col[j])
        coef[mine] = jnp.where(pivot, -1.0, coef[mine])
        for k in range(j + 1, width + 1):
            row = row_bcast(col[k][mine], at)
            old = list(col[k])
            old[mine] = jnp.where(pivot, 0.0, old[mine])
            if k == j + 1:
                col[k] = [old[g] - (coef[g] * row) * inv for g in range(PANEL)]
            else:
                row = row * inv
                col[k] = [old[g] - coef[g] * row for g in range(PANEL)]
    panel = col[width]
    out = list(m)
    for i, g in enumerate(own):
        out[g] = panel[i]
    n = len(m)
    after = range(PANEL * (p + 1), min(n, PANEL * (p + 2)))
    rows = [row_bcast(panel[j // GROUP], j % GROUP) for j in range(width)]
    for g in after:
        out[g] = jnp.where(here, 0.0, m[g]) - tree_sum(
            lane_bcast(m[g], base + j) * rows[j] for j in range(width)
        )
    rest = [g for g in range(n) if g not in own and g not in after]
    right = [jnp.zeros((base, LANES), f32)] if base else []
    right += panel
    if base + width < LANES:
        right.append(jnp.zeros((LANES - base - width, LANES), f32))
    change = dot_exact(
        jnp.concatenate([m[g] for g in rest], axis=0), jnp.concatenate(right, axis=0)
    )
    for t, g in enumerate(rest):
        out[g] = jnp.where(here, 0.0, m[g]) - change[GROUP * t : GROUP * (t + 1)]
    return out


def inverse_128(block, zeros):
    m = [block[GROUP * g : GROUP * (g + 1), :] for g in range(LANES // GROUP)]
    for p in range(LANES // (GROUP * PANEL)):
        m = eliminate(m, p, zeros)
    return jnp.concatenate(m, axis=0)


def ring_taper(first, second, extent, inv_width):
    gap = jnp.abs(first - second)
    gap = jnp.minimum(gap, extent - gap)
    return jnp.maximum(0.0, 1.0 - gap * inv_width)


def down(row, n):
    return jnp.broadcast_to(row, (LANES, n)).T


def obs_place(owner, location, width, lines):
    row = owner * lines + (location // width) % lines
    return row.astype(f32), (location % width).astype(f32)


def inverse_of(scalar):
    return pltpu.reciprocal(jnp.full((1, LANES), scalar.astype(f32), f32))


def across(row, fn):
    return jnp.concatenate(
        [fn(row[:, t : t + LANES]) for t in range(0, row.shape[1], LANES)], axis=1
    )


def solve_kernel(
    owner, widths, gathered, location, values, noise, variance, zero,
    anom_out, weight_out, pred, cov, rhs, *, extents, lines, picked_rows
):
    blocks, members, count = noise.shape
    rows_all, cols_all = extents
    tiles = count // LANES
    scale = 1.0 / (members - 1)
    senders = gathered.shape[0] // (blocks * picked_rows)
    per = members // senders
    zeros = zero[...]
    for b in range(blocks):
        for s in range(senders):
            for t in range(tiles):
                pred[b, s * per : (s + 1) * per, t * LANES : (t + 1) * LANES] = gathered[
                    pl.ds((s * blocks + b) * picked_rows + t, per, stride=tiles), :
                ]

    def taper(b, c):
        row_b, col_b = obs_place(owner[b], location[pl.ds(b, 1), :], cols_all, lines)
        row_c, col_c = obs_place(owner[c], location[pl.ds(c, 1), :], cols_all, lines)
        row_b, col_b = down(row_b, count), down(col_b, count)
        inv_row, inv_col = inverse_of(widths[b, 0]), inverse_of(widths[b, 1])
        return across(row_c, lambda x: ring_taper(row_b, x, float(rows_all), inv_row)) * across(
            col_c, lambda x: ring_taper(col_b, x, float(cols_all), inv_col)
        )

    def block(b, carry):
        now = pred[b]
        anom = now - jnp.sum(now, axis=0, keepdims=True) * (1.0 / members)
        anom_out[b] = anom
        spread = dot_exact(anom.T, anom) * scale
        diag = lax.broadcasted_iota(jnp.int32, (count, count), 0) == lax.broadcasted_iota(
            jnp.int32, (count, count), 1
        )
        cov[...] = taper(b, b) * spread + jnp.where(diag, variance[pl.ds(b, 1), :], 0.0)
        rhs[...] = values[pl.ds(b, 1), :] + noise[b] - now
        corner = cov[0:LANES, 0:LANES]
        for k in range(tiles):
            at = slice(k * LANES, (k + 1) * LANES)
            inv = inverse_128(corner, zeros)
            if k + 1 < tiles:
                after = slice((k + 1) * LANES, count)
                soon = slice((k + 1) * LANES, (k + 2) * LANES)
                low_soon = dot_exact(cov[soon, at], inv)
                corner = cov[soon, soon] - dot_exact(low_soon, cov[at, soon])
                if k + 2 < tiles:
                    late = slice((k + 2) * LANES, count)
                    low_late = dot_exact(cov[late, at], inv)
                    cov[soon, late] -= dot_exact(low_soon, cov[at, late])
                    cov[late, after] -= dot_exact(low_late, cov[at, after])
                    cov[late, at] = low_late
                top = dot_exact(rhs[:, at], inv)
                rhs[:, at] = top
                rhs[:, after] -= dot_exact(top, cov[at, after])
                cov[soon, at] = low_soon
            else:
                rhs[:, at] = dot_exact(rhs[:, at], inv)
        for k in reversed(range(tiles - 1)):
            at = slice(k * LANES, (k + 1) * LANES)
            after = slice((k + 1) * LANES, count)
            rhs[:, at] -= dot_exact(rhs[:, after], cov[after, at])
        weight = rhs[...]
        weight_out[b] = weight

        def later(c, carry):
            now = pred[c]
            anom_c = now - jnp.sum(now, axis=0, keepdims=True) * (1.0 / members)
            left = stacked(anom_out[b]).T.astype(bf16)
            cross = taper(b, c) * (dot_stacked(left, anom_c) * scale)
            pred[c] = now + dot_split(weight_out[b], cross)
            return carry

        lax.fori_loop(b + 1, blocks, later, 0)
        return carry

    lax.fori_loop(0, blocks, block, 0)


def solve(owner, widths, gathered, location, values, noise, variance, extents, lines, picked_rows):
    blocks, members, count = noise.shape
    out = jax.ShapeDtypeStruct((blocks, members, count), f32)

    def body(*refs):
        solve_kernel(*refs, extents=extents, lines=lines, picked_rows=picked_rows)

    return pl.pallas_call(
        body,
        out_shape=[out, out],
        in_specs=[smem, smem] + [vmem] * 6,
        out_specs=[vmem, vmem],
        scratch_shapes=[
            pltpu.VMEM((blocks, members, count), f32),
            pltpu.VMEM((count, count), f32),
            pltpu.VMEM((members, count), f32),
        ],
        compiler_params=params,
        name="solve",
    )(owner, widths, gathered, location, values, noise, variance, jnp.zeros((GROUP, LANES), f32))


def update_kernel(owner, widths, my_row, state, location, anom, weight, out, *, extents, lines):
    rows_all, cols_all = extents
    blocks, members, count = anom.shape
    tiles = state.shape[0] // members
    for t in range(tiles):
        out[:, t * LANES : (t + 1) * LANES] = state[pl.ds(t, members, stride=tiles), :]
    row = my_row[0].astype(f32)
    for b in range(blocks):
        now = out[...]
        centered = now - jnp.sum(now, axis=0, keepdims=True) * (1.0 / members)
        cross = dot_stacked(stacked(anom[b]).T.astype(bf16), centered)
        obs_row, obs_col = obs_place(owner[b], location[b : b + 1, :], cols_all, lines)
        obs_col = down(obs_col, count)
        lane = lax.broadcasted_iota(jnp.int32, (1, tiles * LANES), 1).astype(f32)
        inv_row, inv_col = inverse_of(widths[b, 0]), inverse_of(widths[b, 1])
        by_row = across(obs_row, lambda x: ring_taper(row, x, float(rows_all), inv_row))
        by_col = across(lane, lambda x: ring_taper(obs_col, x, float(cols_all), inv_col))
        out[...] = now + dot_split(weight[b] * (by_row * (1.0 / (members - 1))), by_col * cross)


def update(owner, widths, my_row, state, location, anom, weight, extents, lines):
    blocks, members, count = anom.shape
    tiles = state.shape[0] // members

    def body(*refs):
        update_kernel(*refs, extents=extents, lines=lines)

    return pl.pallas_call(
        body,
        out_shape=jax.ShapeDtypeStruct((members, tiles * LANES), f32),
        in_specs=[smem] * 3 + [vmem] * 4,
        out_specs=vmem,
        compiler_params=params,
        name="update",
    )(owner, widths, my_row, state, location, anom, weight)


def choose_kernel(owner, received, out):
    for b in range(out.shape[0]):
        out[b] = received[owner[b]]


def choose(owner, received):
    return pl.pallas_call(
        choose_kernel,
        out_shape=jax.ShapeDtypeStruct(owner.shape + received.shape[1:], f32),
        in_specs=[smem, vmem],
        out_specs=vmem,
        compiler_params=params,
        name="choose",
    )(owner, received)


def shards(
    starting_sample_set, block_owner, obs_location, taper_pairs, obs_values, obs_noise, obs_variance
):
    members, fields, lines, width = starting_sample_set.shape
    regions = lax.axis_size("reg")
    senders = lax.axis_size("mem")
    region = lax.axis_index("reg")
    mem_index = lax.axis_index("mem")
    extents = (lines * regions, width)
    assert fields * lines == senders

    forth = [(i, (i + 1) % regions) for i in range(regions)]
    back = [((i + 1) % regions, i) for i in range(regions)]
    above = lax.ppermute(starting_sample_set, "reg", forth)
    below = lax.ppermute(starting_sample_set, "reg", back)

    mine = jnp.argmax((block_owner == region).astype(jnp.int32))
    loc = lax.dynamic_slice_in_dim(obs_location, mine, 1, axis=0)
    state, picked = forecast(above, starting_sample_set, below, loc, regions)

    picked_rows = picked.shape[0] // regions
    picked = lax.all_to_all(
        picked.reshape(regions, picked_rows, LANES), "reg", 0, 0, tiled=True
    )
    gathered = lax.all_gather(choose(block_owner, picked), "mem").reshape(-1, LANES)

    state = lax.all_to_all(
        state.reshape(senders, members * GROUP, LANES), "mem", 0, 0, tiled=True
    ).reshape(senders * members * GROUP, LANES)

    anom, weight = solve(
        block_owner, taper_pairs, gathered, obs_location, obs_values, obs_noise, obs_variance,
        extents, lines, picked_rows,
    )
    my_row = (region * lines + mem_index % lines).reshape(1)
    return update(
        block_owner, taper_pairs, my_row, state, obs_location, anom, weight, extents, lines
    )


def solution(mesh):
    return jax.shard_map(
        shards,
        mesh=mesh,
        in_specs=(P("mem", None, "reg", None), P(), P(), P(), P(), P(), P()),
        out_specs=P(None, ("reg", "mem")),
        check_vma=False,
    )
```

```python
import jax
import jax.numpy as jnp
from jax import lax
from jax.experimental import pallas as pl
from jax.experimental.pallas import tpu as pltpu
from jax.sharding import PartitionSpec as P

STEPS = 4
MIX = 0.1
COURANT = 0.05
ROTATION = 0.02
LANES = 128
GROUP = 8
PANEL = 2
highest = lax.Precision.HIGHEST
f32 = jnp.float32
bf16 = jnp.bfloat16

vmem = pl.BlockSpec(memory_space=pltpu.VMEM)
smem = pl.BlockSpec(memory_space=pltpu.SMEM)
params = pltpu.CompilerParams(vmem_limit_bytes=32 * 1024 * 1024)


def dot_exact(a, b):
    return lax.dot_general(
        a, b, (((1,), (0,)), ((), ())), precision=highest, preferred_element_type=f32
    )


def dot_bf16(a, b):
    return lax.dot_general(a, b, (((1,), (0,)), ((), ())), preferred_element_type=f32)


def halves(x):
    hi = x.astype(bf16)
    return hi, (x - hi.astype(f32)).astype(bf16)


def thirds(x):
    hi = x.astype(bf16)
    rest = x - hi.astype(f32)
    mid = rest.astype(bf16)
    return hi, mid, (rest - mid.astype(f32)).astype(bf16)


def dot_split(a, b):
    a_hi, a_lo = halves(a)
    b_hi, b_lo = halves(b)
    return dot_bf16(
        jnp.concatenate([a_hi, a_hi, a_lo], axis=1), jnp.concatenate([b_hi, b_lo, b_hi], axis=0)
    )


def stacked(x):
    hi = x.astype(bf16).astype(f32)
    lo = x - hi
    return jnp.concatenate([hi, hi, lo], axis=0)


def dot_stacked(left, b):
    b_hi, b_lo = halves(b)
    return dot_bf16(left, jnp.concatenate([b_hi, b_lo, b_hi], axis=0))


def tree_sum(terms):
    terms = list(terms)
    while len(terms) > 1:
        terms = [
            terms[i] + terms[i + 1] if i + 1 < len(terms) else terms[i]
            for i in range(0, len(terms), 2)
        ]
    return terms[0]


def forecast_kernel(
    above, own, below, loc, state_out, picked_out, rows, columns, *, picked_rows
):
    members, fields, lines, width = own.shape
    pad = rows.shape[2]
    n_rows = fields * lines * GROUP
    rows[:, :, 0:lines, :] = above[...]
    rows[:, :, lines : 2 * lines, :] = own[...]
    rows[:, :, 2 * lines : 3 * lines, :] = below[...]
    rows[:, :, 3 * lines : pad, :] = jnp.zeros((members, fields, pad - 3 * lines, width), f32)
    columns[...] = jnp.zeros(columns.shape, f32)

    def member(m, carry):
        c = [rows[m, f] for f in range(fields)]
        for _ in range(STEPS):
            n = [pltpu.roll(x, 1, 0) for x in c]
            s = [pltpu.roll(x, pad - 1, 0) for x in c]
            w = [pltpu.roll(x, 1, 1) for x in c]
            e = [pltpu.roll(x, width - 1, 1) for x in c]
            smooth = [
                (1.0 - MIX) * c[f] + MIX * 0.25 * (n[f] + s[f] + w[f] + e[f]) for f in range(fields)
            ]
            dc = [e[f] - w[f] for f in range(fields)]
            dr = [s[f] - n[f] for f in range(fields)]
            carried = [c[1] * dc[f] + c[2] * dr[f] for f in range(fields)]
            flux = (
                (1.0 + e[0]) * e[1]
                - (1.0 + w[0]) * w[1]
                + (1.0 + s[0]) * s[2]
                - (1.0 + n[0]) * n[2]
            )
            c = [
                smooth[0] - COURANT * flux,
                smooth[1] - COURANT * (carried[1] + dc[0]) + ROTATION * c[2],
                smooth[2] - COURANT * (carried[2] + dr[0]) - ROTATION * c[1],
                smooth[3] - COURANT * carried[3],
            ]
        for f in range(fields):
            mine = c[f][lines : 2 * lines]
            for t in range(width // LANES):
                at = t * n_rows + f * lines * GROUP + m
                columns[pl.ds(at, lines, stride=GROUP), :] = mine[:, t * LANES : (t + 1) * LANES]
                at = f * lines * members * GROUP + m * GROUP + t
                state_out[pl.ds(at, lines, stride=members * GROUP), :] = mine[
                    :, t * LANES : (t + 1) * LANES
                ]
        return carry

    lax.fori_loop(0, members, member, 0)

    where = loc[...]
    count = where.shape[1]
    column = where % width
    line = where // width
    onehot = (lax.broadcasted_iota(jnp.int32, (width, count), 0) == column).astype(f32).astype(bf16)
    parts = thirds(
        jnp.concatenate(
            [columns[t * n_rows : (t + 1) * n_rows, :] for t in range(width // LANES)], axis=1
        )
    )
    taken = dot_bf16(jnp.concatenate(parts, axis=0), onehot)
    taken = taken[:n_rows] + taken[n_rows : 2 * n_rows] + taken[2 * n_rows :]
    picked = tree_sum(
        jnp.where(line == d, taken[d * GROUP : (d + 1) * GROUP], 0.0)
        for d in range(fields * lines)
    )[:members]
    chunks = count // LANES
    for r in range(picked_out.shape[0] // picked_rows):
        for t in range(chunks):
            picked_out[pl.ds(r * picked_rows + t, members, stride=chunks), :] = picked[
                :, t * LANES : (t + 1) * LANES
            ]


def forecast(above, own, below, loc, regions):
    members, fields, lines, width = own.shape
    assert width == GROUP * LANES and members <= GROUP
    n_dest = fields * lines
    picked_rows = -(-members * loc.shape[1] // (LANES * GROUP)) * GROUP

    def body(*refs):
        forecast_kernel(*refs, picked_rows=picked_rows)

    return pl.pallas_call(
        body,
        out_shape=[
            jax.ShapeDtypeStruct((n_dest * members * GROUP, LANES), f32),
            jax.ShapeDtypeStruct((regions * picked_rows, LANES), f32),
        ],
        in_specs=[vmem] * 4,
        out_specs=[vmem] * 2,
        scratch_shapes=[
            pltpu.VMEM((members, fields, 4 * lines, width), f32),
            pltpu.VMEM((n_dest * GROUP * GROUP, LANES), f32),
        ],
        compiler_params=params,
        name="forecast",
    )(above, own, below, loc)


def lane_bcast(x, j):
    return jnp.broadcast_to(x[:, j : j + 1], x.shape)


def row_bcast(x, j):
    return jnp.broadcast_to(x[j : j + 1, :], x.shape)


def eliminate(m, p, zeros):
    width = PANEL * GROUP
    lane = lax.broadcasted_iota(jnp.int32, (GROUP, LANES), 1)
    sub = lax.broadcasted_iota(jnp.int32, (GROUP, LANES), 0)
    base = width * p
    here = (lane >= base) & (lane < base + width)
    own = range(PANEL * p, PANEL * (p + 1))
    col = [[lane_bcast(m[g], base + j) + zeros for g in own] for j in range(width)]
    col.append(
        [
            jnp.where(here, (lane - base == sub + GROUP * i).astype(f32), m[g])
            for i, g in enumerate(own)
        ]
    )
    for j in range(width):
        mine, at = divmod(j, GROUP)
        inv = pltpu.reciprocal(row_bcast(col[j][mine], at))
        pivot = sub == at
        coef = list(col[j])
        coef[mine] = jnp.where(pivot, -1.0, coef[mine])
        for k in range(j + 1, width + 1):
            row = row_bcast(col[k][mine], at)
            old = list(col[k])
            old[mine] = jnp.where(pivot, 0.0, old[mine])
            if k == j + 1:
                col[k] = [old[g] - (coef[g] * row) * inv for g in range(PANEL)]
            else:
                row = row * inv
                col[k] = [old[g] - coef[g] * row for g in range(PANEL)]
    panel = col[width]
    out = list(m)
    for i, g in enumerate(own):
        out[g] = panel[i]
    n = len(m)
    after = range(PANEL * (p + 1), min(n, PANEL * (p + 2)))
    rows = [row_bcast(panel[j // GROUP], j % GROUP) for j in range(width)]
    for g in after:
        out[g] = jnp.where(here, 0.0, m[g]) - tree_sum(
            lane_bcast(m[g], base + j) * rows[j] for j in range(width)
        )
    rest = [g for g in range(n) if g not in own and g not in after]
    right = [jnp.zeros((base, LANES), f32)] if base else []
    right += panel
    if base + width < LANES:
        right.append(jnp.zeros((LANES - base - width, LANES), f32))
    change = dot_exact(
        jnp.concatenate([m[g] for g in rest], axis=0), jnp.concatenate(right, axis=0)
    )
    for t, g in enumerate(rest):
        out[g] = jnp.where(here, 0.0, m[g]) - change[GROUP * t : GROUP * (t + 1)]
    return out


def inverse_128(block, zeros):
    m = [block[GROUP * g : GROUP * (g + 1), :] for g in range(LANES // GROUP)]
    for p in range(LANES // (GROUP * PANEL)):
        m = eliminate(m, p, zeros)
    return jnp.concatenate(m, axis=0)


def ring_taper(first, second, extent, inv_width):
    gap = jnp.abs(first - second)
    gap = jnp.minimum(gap, extent - gap)
    return jnp.maximum(0.0, 1.0 - gap * inv_width)


def down(row, n):
    return jnp.broadcast_to(row, (LANES, n)).T


def obs_place(owner, location, width, lines):
    row = owner * lines + (location // width) % lines
    return row.astype(f32), (location % width).astype(f32)


def inverse_of(scalar):
    return pltpu.reciprocal(jnp.full((1, LANES), scalar.astype(f32), f32))


def across(row, fn):
    return jnp.concatenate(
        [fn(row[:, t : t + LANES]) for t in range(0, row.shape[1], LANES)], axis=1
    )


def prepare_kernel(owner, region, location, own, loc, own_copy):
    own_copy[...] = own[...]
    mine = location[0:1, :]
    for b in range(1, location.shape[0]):
        mine = jnp.where(owner[b] == region[0], location[b : b + 1, :], mine)
    loc[...] = mine


def prepare(owner, region, location, own):
    return pl.pallas_call(
        prepare_kernel,
        out_shape=[
            jax.ShapeDtypeStruct((1, location.shape[1]), jnp.int32),
            jax.ShapeDtypeStruct(own.shape, f32),
        ],
        in_specs=[smem] * 2 + [vmem] * 2,
        out_specs=[vmem] * 2,
        compiler_params=params,
        name="prepare",
    )(owner, region, location, own)


def obs_taper(owner, widths, location, b, c, extents, lines):
    rows_all, cols_all = extents
    row_b, col_b = obs_place(owner[b], location[pl.ds(b, 1), :], cols_all, lines)
    row_c, col_c = obs_place(owner[c], location[pl.ds(c, 1), :], cols_all, lines)
    row_b, col_b = down(row_b, row_b.shape[1]), down(col_b, col_b.shape[1])
    inv_row, inv_col = inverse_of(widths[b, 0]), inverse_of(widths[b, 1])
    return across(row_c, lambda x: ring_taper(row_b, x, float(rows_all), inv_row)) * across(
        col_c, lambda x: ring_taper(col_b, x, float(cols_all), inv_col)
    )


def anomaly(x):
    return x - jnp.sum(x, axis=0, keepdims=True) * (1.0 / x.shape[0])


def unpack(gathered, first, senders, stride, per, tiles, out, b):
    for s in range(senders):
        for t in range(tiles):
            out[b, s * per : (s + 1) * per, t * LANES : (t + 1) * LANES] = gathered[
                pl.ds(s * stride + first + t, per, stride=tiles), :
            ]


def weights_of(now, taper, misfit, variance, zeros, cov, rhs):
    members, count = now.shape
    tiles = count // LANES
    anom = anomaly(now)
    spread = dot_exact(anom.T, anom) * (1.0 / (members - 1))
    diag = lax.broadcasted_iota(jnp.int32, (count, count), 0) == lax.broadcasted_iota(
        jnp.int32, (count, count), 1
    )
    cov[...] = taper * spread + jnp.where(diag, variance, 0.0)
    rhs[...] = misfit
    corner = cov[0:LANES, 0:LANES]
    for k in range(tiles):
        at = slice(k * LANES, (k + 1) * LANES)
        inv = inverse_128(corner, zeros)
        if k + 1 < tiles:
            after = slice((k + 1) * LANES, count)
            soon = slice((k + 1) * LANES, (k + 2) * LANES)
            low_soon = dot_exact(cov[soon, at], inv)
            corner = cov[soon, soon] - dot_exact(low_soon, cov[at, soon])
            if k + 2 < tiles:
                late = slice((k + 2) * LANES, count)
                low_late = dot_exact(cov[late, at], inv)
                cov[soon, late] -= dot_exact(low_soon, cov[at, late])
                cov[late, after] -= dot_exact(low_late, cov[at, after])
                cov[late, at] = low_late
            top = dot_exact(rhs[:, at], inv)
            rhs[:, at] = top
            rhs[:, after] -= dot_exact(top, cov[at, after])
            cov[soon, at] = low_soon
        else:
            rhs[:, at] = dot_exact(rhs[:, at], inv)
    for k in reversed(range(tiles - 1)):
        at = slice(k * LANES, (k + 1) * LANES)
        after = slice((k + 1) * LANES, count)
        rhs[:, at] -= dot_exact(rhs[:, after], cov[after, at])
    return anom, rhs[...]


def first_kernel(
    owner, widths, gathered, location, values, noise, variance, zero,
    anom_out, weight_out, pred, cov, rhs, *, senders, extents, lines
):
    members, count = anom_out.shape
    taper = obs_taper(owner, widths, location, 0, 0, extents, lines)
    unpack(gathered, 0, senders, gathered.shape[0] // senders, members // senders, count // LANES, pred, 0)
    now = pred[0]
    anom_out[...], weight_out[...] = weights_of(
        now, taper, values[0:1, :] + noise[0] - now, variance[0:1, :], zero[...], cov, rhs
    )


def rest_kernel(
    owner, widths, gathered, location, values, noise, variance, zero, anom_first, weight_first,
    anom_out, weight_out, pred, cov, rhs, *, senders, extents, lines, skip, picked_rows
):
    blocks, members, count = noise.shape
    tiles = count // LANES
    stride = gathered.shape[0] // senders
    for b in range(1, blocks):
        unpack(
            gathered, skip + (b - 1) * picked_rows, senders, stride, members // senders, tiles, pred, b
        )
    anom_out[0] = anom_first[...]
    weight_out[0] = weight_first[...]

    def block(b, carry):
        def earlier(a, carry):
            now = pred[b]
            left = stacked(anom_out[a]).T.astype(bf16)
            cross = dot_stacked(left, anomaly(now)) * (1.0 / (members - 1))
            pred[b] = now + dot_split(weight_out[a], obs_taper(owner, widths, location, a, b, extents, lines) * cross)
            return carry

        lax.fori_loop(0, b, earlier, 0)
        now = pred[b]
        anom_out[b], weight_out[b] = weights_of(
            now,
            obs_taper(owner, widths, location, b, b, extents, lines),
            values[pl.ds(b, 1), :] + noise[b] - now,
            variance[pl.ds(b, 1), :],
            zero[...],
            cov,
            rhs,
        )
        return carry

    lax.fori_loop(1, blocks, block, 0)


def solve(kernel, blocks_out, args, count, members, **sizes):
    scratch = blocks_out[0] if blocks_out else 1

    def body(*refs):
        kernel(*refs, **sizes)

    return pl.pallas_call(
        body,
        out_shape=[jax.ShapeDtypeStruct(blocks_out + (members, count), f32)] * 2,
        in_specs=[smem] * 2 + [vmem] * (len(args) - 2),
        out_specs=[vmem] * 2,
        scratch_shapes=[
            pltpu.VMEM((scratch, members, count), f32),
            pltpu.VMEM((count, count), f32),
            pltpu.VMEM((members, count), f32),
        ],
        compiler_params=params,
        name="solve",
    )(*args)


def update_kernel(
    owner, widths, my_row, state, location, anom, weight, out, *, extents, lines, senders
):
    rows_all, cols_all = extents
    blocks, members, count = anom.shape
    tiles = cols_all // LANES
    per = members // senders
    stride = state.shape[0] // senders
    for s in range(senders):
        for t in range(tiles):
            out[s * per : (s + 1) * per, t * LANES : (t + 1) * LANES] = state[
                pl.ds(s * stride + t, per, stride=tiles), :
            ]
    row = my_row[0].astype(f32)
    for b in range(blocks):
        now = out[...]
        cross = dot_stacked(stacked(anom[b]).T.astype(bf16), anomaly(now))
        obs_row, obs_col = obs_place(owner[b], location[b : b + 1, :], cols_all, lines)
        obs_col = down(obs_col, count)
        lane = lax.broadcasted_iota(jnp.int32, (1, cols_all), 1).astype(f32)
        inv_row, inv_col = inverse_of(widths[b, 0]), inverse_of(widths[b, 1])
        by_row = across(obs_row, lambda x: ring_taper(row, x, float(rows_all), inv_row))
        by_col = across(lane, lambda x: ring_taper(obs_col, x, float(cols_all), inv_col))
        out[...] = now + dot_split(weight[b] * (by_row * (1.0 / (members - 1))), by_col * cross)


def update(owner, widths, my_row, state, location, anom, weight, extents, lines, senders):
    members = anom.shape[1]

    def body(*refs):
        update_kernel(*refs, extents=extents, lines=lines, senders=senders)

    return pl.pallas_call(
        body,
        out_shape=jax.ShapeDtypeStruct((members, extents[1]), f32),
        in_specs=[smem] * 3 + [vmem] * 4,
        out_specs=vmem,
        compiler_params=params,
        name="update",
    )(owner, widths, my_row, state, location, anom, weight)


def choose_kernel(owner, received, state, first, second):
    receivers, rows, _ = first.shape
    own_rows = state.shape[0] // receivers
    blocks = owner.shape[0]
    chunk = [received[owner[b]] for b in range(blocks)]
    for m in range(receivers):
        first[m] = chunk[0]
        second[m, 0:own_rows, :] = state[m * own_rows : (m + 1) * own_rows, :]
        for b in range(1, blocks):
            at = own_rows + (b - 1) * rows
            second[m, at : at + rows, :] = chunk[b]


def choose(owner, received, state, receivers):
    rows = received.shape[1]
    blocks = owner.shape[0]
    own_rows = state.shape[0] // receivers
    return pl.pallas_call(
        choose_kernel,
        out_shape=[
            jax.ShapeDtypeStruct((receivers, rows, LANES), f32),
            jax.ShapeDtypeStruct((receivers, own_rows + (blocks - 1) * rows, LANES), f32),
        ],
        in_specs=[smem, vmem, vmem],
        out_specs=[vmem, vmem],
        compiler_params=params,
        name="choose",
    )(owner, received, state)


def shards(
    starting_sample_set, block_owner, obs_location, taper_pairs, obs_values, obs_noise, obs_variance
):
    members, fields, lines, width = starting_sample_set.shape
    regions = lax.axis_size("reg")
    senders = lax.axis_size("mem")
    region = lax.axis_index("reg")
    mem_index = lax.axis_index("mem")
    extents = (lines * regions, width)
    assert fields * lines == senders

    forth = [(i, (i + 1) % regions) for i in range(regions)]
    back = [((i + 1) % regions, i) for i in range(regions)]
    above = lax.ppermute(starting_sample_set, "reg", forth)
    below = lax.ppermute(starting_sample_set, "reg", back)

    loc, own = prepare(block_owner, region.reshape(1), obs_location, starting_sample_set)
    state, picked = forecast(above, own, below, loc, regions)

    picked_rows = picked.shape[0] // regions
    picked = lax.all_to_all(
        picked.reshape(regions, picked_rows, LANES), "reg", 0, 0, tiled=True
    )
    skip = members * GROUP
    first, second = choose(block_owner, picked, state, senders)
    first = lax.all_to_all(first, "mem", 0, 0, tiled=True)
    first, second = lax.optimization_barrier((first, second))
    second = lax.all_to_all(second, "mem", 0, 0, tiled=True).reshape(-1, LANES)

    zero = jnp.zeros((GROUP, LANES), f32)
    sizes = dict(count=obs_location.shape[1], members=obs_noise.shape[1], senders=senders)
    sizes.update(extents=extents, lines=lines)
    common = (obs_location, obs_values, obs_noise, obs_variance, zero)
    done = solve(
        first_kernel, (), (block_owner, taper_pairs, first.reshape(-1, LANES)) + common, **sizes
    )
    anom, weight = solve(
        rest_kernel, block_owner.shape, (block_owner, taper_pairs, second) + common + tuple(done),
        skip=skip, picked_rows=picked_rows, **sizes,
    )
    my_row = (region * lines + mem_index % lines).reshape(1)
    return update(
        block_owner, taper_pairs, my_row, second, obs_location, anom, weight, extents, lines, senders
    )


def solution(mesh):
    return jax.shard_map(
        shards,
        mesh=mesh,
        in_specs=(P("mem", None, "reg", None), P(), P(), P(), P(), P(), P()),
        out_specs=P(None, ("reg", "mem")),
        check_vma=False,
    )
```

```python
import jax
import jax.numpy as jnp
from jax import lax
from jax.experimental import pallas as pl
from jax.experimental.pallas import tpu as pltpu
from jax.sharding import PartitionSpec as P

STEPS = 4
MIX = 0.1
COURANT = 0.05
ROTATION = 0.02
LANES = 128
GROUP = 8
PANEL = 2
highest = lax.Precision.HIGHEST
f32 = jnp.float32
bf16 = jnp.bfloat16

vmem = pl.BlockSpec(memory_space=pltpu.VMEM)
smem = pl.BlockSpec(memory_space=pltpu.SMEM)
params = pltpu.CompilerParams(vmem_limit_bytes=32 * 1024 * 1024)


def dot_exact(a, b):
    return lax.dot_general(
        a, b, (((1,), (0,)), ((), ())), precision=highest, preferred_element_type=f32
    )


def dot_bf16(a, b):
    return lax.dot_general(a, b, (((1,), (0,)), ((), ())), preferred_element_type=f32)


def halves(x):
    hi = x.astype(bf16)
    return hi, (x - hi.astype(f32)).astype(bf16)


def thirds(x):
    hi = x.astype(bf16)
    rest = x - hi.astype(f32)
    mid = rest.astype(bf16)
    return hi, mid, (rest - mid.astype(f32)).astype(bf16)


def dot_split(a, b):
    a_hi, a_lo = halves(a)
    b_hi, b_lo = halves(b)
    return dot_bf16(
        jnp.concatenate([a_hi, a_hi, a_lo], axis=1), jnp.concatenate([b_hi, b_lo, b_hi], axis=0)
    )


def stacked(x):
    hi = x.astype(bf16).astype(f32)
    lo = x - hi
    return jnp.concatenate([hi, hi, lo], axis=0)


def dot_stacked(left, b):
    b_hi, b_lo = halves(b)
    return dot_bf16(left, jnp.concatenate([b_hi, b_lo, b_hi], axis=0))


def tree_sum(terms):
    terms = list(terms)
    while len(terms) > 1:
        terms = [
            terms[i] + terms[i + 1] if i + 1 < len(terms) else terms[i]
            for i in range(0, len(terms), 2)
        ]
    return terms[0]


def forecast_kernel(
    above, own, below, loc, state_out, picked_out, rows, columns, *, picked_rows
):
    members, fields, lines, width = own.shape
    pad = rows.shape[2]
    n_rows = fields * lines * GROUP
    rows[:, :, 0:lines, :] = above[...]
    rows[:, :, lines : 2 * lines, :] = own[...]
    rows[:, :, 2 * lines : 3 * lines, :] = below[...]
    rows[:, :, 3 * lines : pad, :] = jnp.zeros((members, fields, pad - 3 * lines, width), f32)
    columns[...] = jnp.zeros(columns.shape, f32)

    def member(m, carry):
        c = [rows[m, f] for f in range(fields)]
        first = 0
        for step in range(STEPS):
            if 3 * lines - 2 * step == GROUP:
                c = [x[step : step + GROUP] for x in c]
                first = step
            n = [pltpu.roll(x, 1, 0) for x in c]
            s = [pltpu.roll(x, x.shape[0] - 1, 0) for x in c]
            w = [pltpu.roll(x, 1, 1) for x in c]
            e = [pltpu.roll(x, width - 1, 1) for x in c]
            smooth = [
                (1.0 - MIX) * c[f] + MIX * 0.25 * (n[f] + s[f] + w[f] + e[f]) for f in range(fields)
            ]
            dc = [e[f] - w[f] for f in range(fields)]
            dr = [s[f] - n[f] for f in range(fields)]
            carried = [c[1] * dc[f] + c[2] * dr[f] for f in range(fields)]
            flux = (
                (1.0 + e[0]) * e[1]
                - (1.0 + w[0]) * w[1]
                + (1.0 + s[0]) * s[2]
                - (1.0 + n[0]) * n[2]
            )
            c = [
                smooth[0] - COURANT * flux,
                smooth[1] - COURANT * (carried[1] + dc[0]) + ROTATION * c[2],
                smooth[2] - COURANT * (carried[2] + dr[0]) - ROTATION * c[1],
                smooth[3] - COURANT * carried[3],
            ]
        for f in range(fields):
            mine = c[f][lines - first : 2 * lines - first]
            for t in range(width // LANES):
                at = t * n_rows + f * lines * GROUP + m
                columns[pl.ds(at, lines, stride=GROUP), :] = mine[:, t * LANES : (t + 1) * LANES]
                at = f * lines * members * GROUP + m * GROUP + t
                state_out[pl.ds(at, lines, stride=members * GROUP), :] = mine[
                    :, t * LANES : (t + 1) * LANES
                ]
        return carry

    lax.fori_loop(0, members, member, 0)

    where = loc[...]
    count = where.shape[1]
    column = where % width
    line = where // width
    onehot = (lax.broadcasted_iota(jnp.int32, (width, count), 0) == column).astype(f32).astype(bf16)
    parts = thirds(
        jnp.concatenate(
            [columns[t * n_rows : (t + 1) * n_rows, :] for t in range(width // LANES)], axis=1
        )
    )
    taken = dot_bf16(jnp.concatenate(parts, axis=0), onehot)
    taken = taken[:n_rows] + taken[n_rows : 2 * n_rows] + taken[2 * n_rows :]
    picked = tree_sum(
        jnp.where(line == d, taken[d * GROUP : (d + 1) * GROUP], 0.0)
        for d in range(fields * lines)
    )[:members]
    chunks = count // LANES
    for r in range(picked_out.shape[0] // picked_rows):
        for t in range(chunks):
            picked_out[pl.ds(r * picked_rows + t, members, stride=chunks), :] = picked[
                :, t * LANES : (t + 1) * LANES
            ]


def forecast(above, own, below, loc, regions):
    members, fields, lines, width = own.shape
    assert width == GROUP * LANES and members <= GROUP
    n_dest = fields * lines
    picked_rows = -(-members * loc.shape[1] // (LANES * GROUP)) * GROUP

    def body(*refs):
        forecast_kernel(*refs, picked_rows=picked_rows)

    return pl.pallas_call(
        body,
        out_shape=[
            jax.ShapeDtypeStruct((n_dest * members * GROUP, LANES), f32),
            jax.ShapeDtypeStruct((regions * picked_rows, LANES), f32),
        ],
        in_specs=[vmem] * 4,
        out_specs=[vmem] * 2,
        scratch_shapes=[
            pltpu.VMEM((members, fields, 4 * lines, width), f32),
            pltpu.VMEM((n_dest * GROUP * GROUP, LANES), f32),
        ],
        compiler_params=params,
        name="forecast",
    )(above, own, below, loc)


def lane_bcast(x, j):
    return jnp.broadcast_to(x[:, j : j + 1], x.shape)


def row_bcast(x, j):
    return jnp.broadcast_to(x[j : j + 1, :], x.shape)


def eliminate(m, p, zeros):
    width = PANEL * GROUP
    lane = lax.broadcasted_iota(jnp.int32, (GROUP, LANES), 1)
    sub = lax.broadcasted_iota(jnp.int32, (GROUP, LANES), 0)
    base = width * p
    here = (lane >= base) & (lane < base + width)
    own = range(PANEL * p, PANEL * (p + 1))
    col = [[lane_bcast(m[g], base + j) + zeros for g in own] for j in range(width)]
    col.append(
        [
            jnp.where(here, (lane - base == sub + GROUP * i).astype(f32), m[g])
            for i, g in enumerate(own)
        ]
    )
    scale = [None] * PANEL
    for j in range(width):
        mine, at = divmod(j, GROUP)
        pivot = sub == at
        inv = pltpu.reciprocal(row_bcast(col[j][mine], at))
        scale[mine] = inv if scale[mine] is None else jnp.where(pivot, inv, scale[mine])
        coef = list(col[j])
        coef[mine] = jnp.where(pivot, 0.0, coef[mine])
        for k in range(j + 1, width + 1):
            row = row_bcast(col[k][mine], at)
            if k == j + 1:
                col[k] = [col[k][g] - (coef[g] * row) * inv for g in range(PANEL)]
            else:
                row = row * inv
                col[k] = [col[k][g] - coef[g] * row for g in range(PANEL)]
    panel = [col[width][g] * scale[g] for g in range(PANEL)]
    out = list(m)
    for i, g in enumerate(own):
        out[g] = panel[i]
    n = len(m)
    after = range(PANEL * (p + 1), min(n, PANEL * (p + 2)))
    rows = [row_bcast(panel[j // GROUP], j % GROUP) for j in range(width)]
    for g in after:
        out[g] = jnp.where(here, 0.0, m[g]) - tree_sum(
            lane_bcast(m[g], base + j) * rows[j] for j in range(width)
        )
    rest = [g for g in range(n) if g not in own and g not in after]
    right = [jnp.zeros((base, LANES), f32)] if base else []
    right += panel
    if base + width < LANES:
        right.append(jnp.zeros((LANES - base - width, LANES), f32))
    change = dot_exact(
        jnp.concatenate([m[g] for g in rest], axis=0), jnp.concatenate(right, axis=0)
    )
    for t, g in enumerate(rest):
        out[g] = jnp.where(here, 0.0, m[g]) - change[GROUP * t : GROUP * (t + 1)]
    return out


def inverse_128(block, zeros):
    m = [block[GROUP * g : GROUP * (g + 1), :] for g in range(LANES // GROUP)]
    for p in range(LANES // (GROUP * PANEL)):
        m = eliminate(m, p, zeros)
    return jnp.concatenate(m, axis=0)


def ring_taper(first, second, extent, inv_width):
    gap = jnp.abs(first - second)
    gap = jnp.minimum(gap, extent - gap)
    return jnp.maximum(0.0, 1.0 - gap * inv_width)


def down(row, n):
    return jnp.broadcast_to(row, (LANES, n)).T


def obs_place(owner, location, width, lines):
    row = owner * lines + (location // width) % lines
    return row.astype(f32), (location % width).astype(f32)


def inverse_of(scalar):
    return pltpu.reciprocal(jnp.full((1, LANES), scalar.astype(f32), f32))


def across(row, fn):
    return jnp.concatenate(
        [fn(row[:, t : t + LANES]) for t in range(0, row.shape[1], LANES)], axis=1
    )


def prepare_kernel(owner, region, location, own, loc, own_copy):
    own_copy[...] = own[...]
    mine = location[0:1, :]
    for b in range(1, location.shape[0]):
        mine = jnp.where(owner[b] == region[0], location[b : b + 1, :], mine)
    loc[...] = mine


def prepare(owner, region, location, own):
    return pl.pallas_call(
        prepare_kernel,
        out_shape=[
            jax.ShapeDtypeStruct((1, location.shape[1]), jnp.int32),
            jax.ShapeDtypeStruct(own.shape, f32),
        ],
        in_specs=[smem] * 2 + [vmem] * 2,
        out_specs=[vmem] * 2,
        compiler_params=params,
        name="prepare",
    )(owner, region, location, own)


def obs_taper(owner, widths, location, b, c, extents, lines):
    rows_all, cols_all = extents
    row_b, col_b = obs_place(owner[b], location[pl.ds(b, 1), :], cols_all, lines)
    row_c, col_c = obs_place(owner[c], location[pl.ds(c, 1), :], cols_all, lines)
    row_b, col_b = down(row_b, row_b.shape[1]), down(col_b, col_b.shape[1])
    inv_row, inv_col = inverse_of(widths[b, 0]), inverse_of(widths[b, 1])
    return across(row_c, lambda x: ring_taper(row_b, x, float(rows_all), inv_row)) * across(
        col_c, lambda x: ring_taper(col_b, x, float(cols_all), inv_col)
    )


def anomaly(x):
    return x - jnp.sum(x, axis=0, keepdims=True) * (1.0 / x.shape[0])


def unpack(gathered, first, senders, stride, per, tiles, out):
    for s in range(senders):
        for t in range(tiles):
            out[s * per : (s + 1) * per, t * LANES : (t + 1) * LANES] = gathered[
                pl.ds(s * stride + first + t, per, stride=tiles), :
            ]


def weights_of(now, taper, misfit, variance, zeros, cov, rhs, beside=lambda k: None):
    members, count = now.shape
    tiles = count // LANES
    anom = anomaly(now)
    spread = dot_exact(anom.T, anom) * (1.0 / (members - 1))
    diag = lax.broadcasted_iota(jnp.int32, (count, count), 0) == lax.broadcasted_iota(
        jnp.int32, (count, count), 1
    )
    cov[...] = taper * spread + jnp.where(diag, variance, 0.0)
    rhs[...] = misfit
    corner = cov[0:LANES, 0:LANES]
    for k in range(tiles):
        before = slice(0, k * LANES)
        at = slice(k * LANES, (k + 1) * LANES)
        after = slice((k + 1) * LANES, count)
        inv = inverse_128(corner, zeros)
        if k + 1 < tiles:
            soon = slice((k + 1) * LANES, (k + 2) * LANES)
            low_soon = dot_exact(cov[soon, at], inv)
            corner = cov[soon, soon] - dot_exact(low_soon, cov[at, soon])
            low = low_soon
            if k + 2 < tiles:
                late = slice((k + 2) * LANES, count)
                low_late = dot_exact(cov[late, at], inv)
                cov[soon, late] -= dot_exact(low_soon, cov[at, late])
                cov[late, after] -= dot_exact(low_late, cov[at, after])
                low = jnp.concatenate([low_soon, low_late], axis=0)
        top = dot_exact(rhs[:, at], inv)
        rhs[:, at] = top
        if k + 1 < tiles:
            rhs[:, after] -= dot_exact(top, cov[at, after])
            if k:
                cov[after, before] -= dot_exact(low, cov[at, before])
            cov[after, at] = low
        if k:
            rhs[:, before] -= dot_exact(top, cov[at, before])
        beside(k)
    return anom, rhs[...]


def first_kernel(
    owner, widths, gathered, location, values, noise, variance, zero,
    anom_out, weight_out, pred, cov, rhs, *, senders, extents, lines
):
    members, count = anom_out.shape
    taper = obs_taper(owner, widths, location, 0, 0, extents, lines)
    stride = gathered.shape[0] // senders
    unpack(gathered, 0, senders, stride, members // senders, count // LANES, pred)
    now = pred[...]
    anom_out[...], weight_out[...] = weights_of(
        now, taper, values[0:1, :] + noise[0] - now, variance[0:1, :], zero[...], cov, rhs
    )


def rest_kernel(
    owner, widths, gathered, location, values, noise, variance, zero, anom_first, weight_first, my_row,
    out, anom_all, weight_all, pred, cov, rhs, *, senders, extents, lines, skip, picked_rows
):
    rows_all, cols_all = extents
    blocks, members, count = noise.shape
    per = members // senders
    stride = gathered.shape[0] // senders
    for b in range(1, blocks):
        unpack(
            gathered, skip + (b - 1) * picked_rows, senders, stride, per, count // LANES, pred.at[b]
        )
    unpack(gathered, 0, senders, stride, per, cols_all // LANES, out)
    anom_all[0] = anom_first[...]
    weight_all[0] = weight_first[...]
    row = my_row[0].astype(f32)
    share = 1.0 / (members - 1)

    def own_variables(b):
        obs_row, obs_col = obs_place(owner[b], location[pl.ds(b, 1), :], cols_all, lines)
        inv_row, inv_col = inverse_of(widths[b, 0]), inverse_of(widths[b, 1])
        left = stacked(anom_all[b]).T.astype(bf16)
        by_row = across(obs_row, lambda x: ring_taper(row, x, float(rows_all), inv_row))
        weight = weight_all[b] * (by_row * share)
        obs_col = down(obs_col, count)

        def part(k, parts=count // LANES):
            size = cols_all // parts
            at = slice(k * size, (k + 1) * size)
            now = out[:, at]
            cross = dot_stacked(left, anomaly(now))
            lane = lax.broadcasted_iota(jnp.int32, (1, size), 1).astype(f32) + float(k * size)
            by_col = across(lane, lambda x: ring_taper(obs_col, x, float(cols_all), inv_col))
            out[:, at] = now + dot_split(weight, by_col * cross)

        return part

    def block(b, carry):
        def earlier(a, carry):
            now = pred[b]
            left = stacked(anom_all[a]).T.astype(bf16)
            cross = dot_stacked(left, anomaly(now)) * share
            taper = obs_taper(owner, widths, location, a, b, extents, lines)
            pred[b] = now + dot_split(weight_all[a], taper * cross)
            return carry

        lax.fori_loop(0, b, earlier, 0)
        now = pred[b]
        anom, weight = weights_of(
            now,
            obs_taper(owner, widths, location, b, b, extents, lines),
            values[pl.ds(b, 1), :] + noise[b] - now,
            variance[pl.ds(b, 1), :],
            zero[...],
            cov,
            rhs,
            own_variables(b - 1),
        )
        anom_all[b] = anom
        weight_all[b] = weight
        return carry

    lax.fori_loop(1, blocks, block, 0)
    own_variables(blocks - 1)(0, 1)


def solve(kernel, args, outs, scratch, count, members, **sizes):
    def body(*refs):
        kernel(*refs, **sizes)

    return pl.pallas_call(
        body,
        out_shape=[jax.ShapeDtypeStruct(shape, f32) for shape in outs],
        in_specs=[smem] * 2 + [vmem] * 8 + [smem] if len(args) == 11 else [smem] * 2 + [vmem] * 6,
        out_specs=[vmem] * len(outs),
        scratch_shapes=[pltpu.VMEM(shape, f32) for shape in scratch]
        + [pltpu.VMEM((count, count), f32), pltpu.VMEM((members, count), f32)],
        compiler_params=params,
        name="solve",
    )(*args)


def choose_kernel(owner, received, state, first, second, *, used):
    receivers = first.shape[0]
    own_rows = state.shape[0] // receivers
    blocks = owner.shape[0]
    chunk = [received[owner[b]] for b in range(blocks)]
    for m in range(receivers):
        first[m] = chunk[0]
        second[m, 0:own_rows, :] = state[m * own_rows : (m + 1) * own_rows, :]
        for b in range(1, blocks):
            at = own_rows + (b - 1) * used
            second[m, at : at + used, :] = chunk[b][:used]


def choose(owner, received, state, receivers, used):
    rows = received.shape[1]
    blocks = owner.shape[0]
    own_rows = state.shape[0] // receivers

    def body(*refs):
        choose_kernel(*refs, used=used)

    return pl.pallas_call(
        body,
        out_shape=[
            jax.ShapeDtypeStruct((receivers, rows, LANES), f32),
            jax.ShapeDtypeStruct((receivers, own_rows + (blocks - 1) * used, LANES), f32),
        ],
        in_specs=[smem, vmem, vmem],
        out_specs=[vmem, vmem],
        compiler_params=params,
        name="choose",
    )(owner, received, state)


def shards(
    starting_sample_set, block_owner, obs_location, taper_pairs, obs_values, obs_noise, obs_variance
):
    members, fields, lines, width = starting_sample_set.shape
    regions = lax.axis_size("reg")
    senders = lax.axis_size("mem")
    region = lax.axis_index("reg")
    mem_index = lax.axis_index("mem")
    extents = (lines * regions, width)
    assert fields * lines == senders

    forth = [(i, (i + 1) % regions) for i in range(regions)]
    back = [((i + 1) % regions, i) for i in range(regions)]
    above = lax.ppermute(starting_sample_set, "reg", forth)
    below = lax.ppermute(starting_sample_set, "reg", back)

    loc, own = prepare(block_owner, region.reshape(1), obs_location, starting_sample_set)
    state, picked = forecast(above, own, below, loc, regions)

    picked_rows = picked.shape[0] // regions
    picked = lax.all_to_all(
        picked.reshape(regions, picked_rows, LANES), "reg", 0, 0, tiled=True
    )
    skip = members * GROUP
    used = members * obs_location.shape[1] // LANES
    first, second = choose(block_owner, picked, state, senders, used)
    first = lax.all_to_all(first, "mem", 0, 0, tiled=True)
    first, second = lax.optimization_barrier((first, second))
    second = lax.all_to_all(second, "mem", 0, 0, tiled=True).reshape(-1, LANES)

    zero = jnp.zeros((GROUP, LANES), f32)
    my_row = (region * lines + mem_index % lines).reshape(1)
    one = obs_noise.shape[1:]
    sizes = dict(count=one[1], members=one[0], senders=senders, extents=extents, lines=lines)
    common = (obs_location, obs_values, obs_noise, obs_variance, zero)
    done = solve(
        first_kernel,
        (block_owner, taper_pairs, first.reshape(-1, LANES)) + common,
        (one, one),
        (one,),
        **sizes,
    )
    return solve(
        rest_kernel,
        (block_owner, taper_pairs, second) + common + tuple(done) + (my_row,),
        ((one[0], width),),
        (obs_noise.shape,) * 3,
        skip=skip,
        picked_rows=used,
        **sizes,
    )[0]


def solution(mesh):
    return jax.shard_map(
        shards,
        mesh=mesh,
        in_specs=(P("mem", None, "reg", None), P(), P(), P(), P(), P(), P()),
        out_specs=P(None, ("reg", "mem")),
        check_vma=False,
    )
```

```python
import jax
import jax.numpy as jnp
from jax import lax
from jax.experimental import pallas as pl
from jax.experimental.pallas import tpu as pltpu
from jax.sharding import PartitionSpec as P

STEPS = 4
MIX = 0.1
COURANT = 0.05
ROTATION = 0.02
LANES = 128
GROUP = 8
PANEL = 2
highest = lax.Precision.HIGHEST
f32 = jnp.float32
bf16 = jnp.bfloat16

vmem = pl.BlockSpec(memory_space=pltpu.VMEM)
smem = pl.BlockSpec(memory_space=pltpu.SMEM)
params = pltpu.CompilerParams(vmem_limit_bytes=32 * 1024 * 1024)


def dot_exact(a, b):
    return lax.dot_general(
        a, b, (((1,), (0,)), ((), ())), precision=highest, preferred_element_type=f32
    )


def dot_bf16(a, b):
    return lax.dot_general(a, b, (((1,), (0,)), ((), ())), preferred_element_type=f32)


def halves(x):
    hi = x.astype(bf16)
    return hi, (x - hi.astype(f32)).astype(bf16)


def thirds(x):
    hi = x.astype(bf16)
    rest = x - hi.astype(f32)
    mid = rest.astype(bf16)
    return hi, mid, (rest - mid.astype(f32)).astype(bf16)


def dot_split(a, b):
    a_hi, a_lo = halves(a)
    b_hi, b_lo = halves(b)
    return dot_bf16(
        jnp.concatenate([a_hi, a_hi, a_lo], axis=1), jnp.concatenate([b_hi, b_lo, b_hi], axis=0)
    )


def stacked(x):
    hi = x.astype(bf16).astype(f32)
    lo = x - hi
    return jnp.concatenate([hi, hi, lo], axis=0)


def dot_stacked(left, b):
    b_hi, b_lo = halves(b)
    return dot_bf16(left, jnp.concatenate([b_hi, b_lo, b_hi], axis=0))


def tree_sum(terms):
    terms = list(terms)
    while len(terms) > 1:
        terms = [
            terms[i] + terms[i + 1] if i + 1 < len(terms) else terms[i]
            for i in range(0, len(terms), 2)
        ]
    return terms[0]


def forecast_kernel(
    above, own, below, loc, state_out, picked_out, rows, columns, *, picked_rows
):
    members, fields, lines, width = own.shape
    pad = rows.shape[2]
    n_rows = fields * lines * GROUP
    rows[:, :, 0:lines, :] = above[...]
    rows[:, :, lines : 2 * lines, :] = own[...]
    rows[:, :, 2 * lines : 3 * lines, :] = below[...]
    rows[:, :, 3 * lines : pad, :] = jnp.zeros((members, fields, pad - 3 * lines, width), f32)
    columns[...] = jnp.zeros(columns.shape, f32)

    def member(m, carry):
        c = [rows[m, f] for f in range(fields)]
        first = 0
        for step in range(STEPS):
            if 3 * lines - 2 * step == GROUP:
                c = [x[step : step + GROUP] for x in c]
                first = step
            n = [pltpu.roll(x, 1, 0) for x in c]
            s = [pltpu.roll(x, x.shape[0] - 1, 0) for x in c]
            w = [pltpu.roll(x, 1, 1) for x in c]
            e = [pltpu.roll(x, width - 1, 1) for x in c]
            smooth = [
                (1.0 - MIX) * c[f] + MIX * 0.25 * (n[f] + s[f] + w[f] + e[f]) for f in range(fields)
            ]
            dc = [e[f] - w[f] for f in range(fields)]
            dr = [s[f] - n[f] for f in range(fields)]
            carried = [c[1] * dc[f] + c[2] * dr[f] for f in range(fields)]
            flux = (
                (1.0 + e[0]) * e[1]
                - (1.0 + w[0]) * w[1]
                + (1.0 + s[0]) * s[2]
                - (1.0 + n[0]) * n[2]
            )
            c = [
                smooth[0] - COURANT * flux,
                smooth[1] - COURANT * (carried[1] + dc[0]) + ROTATION * c[2],
                smooth[2] - COURANT * (carried[2] + dr[0]) - ROTATION * c[1],
                smooth[3] - COURANT * carried[3],
            ]
        for f in range(fields):
            mine = c[f][lines - first : 2 * lines - first]
            for t in range(width // LANES):
                at = t * n_rows + f * lines * GROUP + m
                columns[pl.ds(at, lines, stride=GROUP), :] = mine[:, t * LANES : (t + 1) * LANES]
                at = f * lines * members * GROUP + m * GROUP + t
                state_out[pl.ds(at, lines, stride=members * GROUP), :] = mine[
                    :, t * LANES : (t + 1) * LANES
                ]
        return carry

    lax.fori_loop(0, members, member, 0, unroll=True)

    where = loc[...]
    count = where.shape[1]
    column = where % width
    line = where // width
    onehot = (lax.broadcasted_iota(jnp.int32, (width, count), 0) == column).astype(f32).astype(bf16)
    parts = thirds(
        jnp.concatenate(
            [columns[t * n_rows : (t + 1) * n_rows, :] for t in range(width // LANES)], axis=1
        )
    )
    taken = dot_bf16(jnp.concatenate(parts, axis=0), onehot)
    taken = taken[:n_rows] + taken[n_rows : 2 * n_rows] + taken[2 * n_rows :]
    picked = tree_sum(
        jnp.where(line == d, taken[d * GROUP : (d + 1) * GROUP], 0.0)
        for d in range(fields * lines)
    )[:members]
    chunks = count // LANES
    for r in range(picked_out.shape[0] // picked_rows):
        for t in range(chunks):
            picked_out[pl.ds(r * picked_rows + t, members, stride=chunks), :] = picked[
                :, t * LANES : (t + 1) * LANES
            ]


def forecast(above, own, below, loc, regions):
    members, fields, lines, width = own.shape
    assert width == GROUP * LANES and members <= GROUP
    n_dest = fields * lines
    picked_rows = -(-members * loc.shape[1] // (LANES * GROUP)) * GROUP

    def body(*refs):
        forecast_kernel(*refs, picked_rows=picked_rows)

    return pl.pallas_call(
        body,
        out_shape=[
            jax.ShapeDtypeStruct((n_dest * members * GROUP, LANES), f32),
            jax.ShapeDtypeStruct((regions * picked_rows, LANES), f32),
        ],
        in_specs=[vmem] * 4,
        out_specs=[vmem] * 2,
        scratch_shapes=[
            pltpu.VMEM((members, fields, 4 * lines, width), f32),
            pltpu.VMEM((n_dest * GROUP * GROUP, LANES), f32),
        ],
        compiler_params=params,
        name="forecast",
    )(above, own, below, loc)


def lane_bcast(x, j):
    return jnp.broadcast_to(x[:, j : j + 1], x.shape)


def row_bcast(x, j):
    return jnp.broadcast_to(x[j : j + 1, :], x.shape)


def eliminate(m, p, zeros):
    width = PANEL * GROUP
    lane = lax.broadcasted_iota(jnp.int32, (GROUP, LANES), 1)
    sub = lax.broadcasted_iota(jnp.int32, (GROUP, LANES), 0)
    base = width * p
    here = (lane >= base) & (lane < base + width)
    own = range(PANEL * p, PANEL * (p + 1))
    col = [[lane_bcast(m[g], base + j) + zeros for g in own] for j in range(width)]
    col.append(
        [
            jnp.where(here, (lane - base == sub + GROUP * i).astype(f32), m[g])
            for i, g in enumerate(own)
        ]
    )
    scale = [None] * PANEL
    for j in range(width):
        mine, at = divmod(j, GROUP)
        pivot = sub == at
        inv = pltpu.reciprocal(row_bcast(col[j][mine], at))
        scale[mine] = inv if scale[mine] is None else jnp.where(pivot, inv, scale[mine])
        coef = list(col[j])
        coef[mine] = jnp.where(pivot, 0.0, coef[mine])
        for k in range(j + 1, width + 1):
            row = row_bcast(col[k][mine], at)
            if k == j + 1:
                col[k] = [col[k][g] - (coef[g] * row) * inv for g in range(PANEL)]
            else:
                row = row * inv
                col[k] = [col[k][g] - coef[g] * row for g in range(PANEL)]
    panel = [col[width][g] * scale[g] for g in range(PANEL)]
    out = list(m)
    for i, g in enumerate(own):
        out[g] = panel[i]
    n = len(m)
    after = range(PANEL * (p + 1), min(n, PANEL * (p + 2)))
    rows = [row_bcast(panel[j // GROUP], j % GROUP) for j in range(width)]
    for g in after:
        out[g] = jnp.where(here, 0.0, m[g]) - tree_sum(
            lane_bcast(m[g], base + j) * rows[j] for j in range(width)
        )
    rest = [g for g in range(n) if g not in own and g not in after]
    right = [jnp.zeros((base, LANES), f32)] if base else []
    right += panel
    if base + width < LANES:
        right.append(jnp.zeros((LANES - base - width, LANES), f32))
    change = dot_exact(
        jnp.concatenate([m[g] for g in rest], axis=0), jnp.concatenate(right, axis=0)
    )
    for t, g in enumerate(rest):
        out[g] = jnp.where(here, 0.0, m[g]) - change[GROUP * t : GROUP * (t + 1)]
    return out


def inverse_128(block, zeros):
    m = [block[GROUP * g : GROUP * (g + 1), :] for g in range(LANES // GROUP)]
    for p in range(LANES // (GROUP * PANEL)):
        m = eliminate(m, p, zeros)
    return jnp.concatenate(m, axis=0)


def ring_taper(first, second, extent, inv_width):
    gap = jnp.abs(first - second)
    gap = jnp.minimum(gap, extent - gap)
    return jnp.maximum(0.0, 1.0 - gap * inv_width)


def down(row, n):
    return jnp.broadcast_to(row, (LANES, n)).T


def obs_place(owner, location, width, lines):
    row = owner * lines + (location // width) % lines
    return row.astype(f32), (location % width).astype(f32)


def inverse_of(scalar):
    return pltpu.reciprocal(jnp.full((1, LANES), scalar.astype(f32), f32))


def across(row, fn):
    return jnp.concatenate(
        [fn(row[:, t : t + LANES]) for t in range(0, row.shape[1], LANES)], axis=1
    )


def prepare_kernel(owner, region, location, own, loc, own_copy):
    own_copy[...] = own[...]
    mine = location[0:1, :]
    for b in range(1, location.shape[0]):
        mine = jnp.where(owner[b] == region[0], location[b : b + 1, :], mine)
    loc[...] = mine


def prepare(owner, region, location, own):
    return pl.pallas_call(
        prepare_kernel,
        out_shape=[
            jax.ShapeDtypeStruct((1, location.shape[1]), jnp.int32),
            jax.ShapeDtypeStruct(own.shape, f32),
        ],
        in_specs=[smem] * 2 + [vmem] * 2,
        out_specs=[vmem] * 2,
        compiler_params=params,
        name="prepare",
    )(owner, region, location, own)


def obs_taper(owner, widths, location, b, c, extents, lines):
    rows_all, cols_all = extents
    row_b, col_b = obs_place(owner[b], location[pl.ds(b, 1), :], cols_all, lines)
    row_c, col_c = obs_place(owner[c], location[pl.ds(c, 1), :], cols_all, lines)
    row_b, col_b = down(row_b, row_b.shape[1]), down(col_b, col_b.shape[1])
    inv_row, inv_col = inverse_of(widths[b, 0]), inverse_of(widths[b, 1])
    return across(row_c, lambda x: ring_taper(row_b, x, float(rows_all), inv_row)) * across(
        col_c, lambda x: ring_taper(col_b, x, float(cols_all), inv_col)
    )


def anomaly(x):
    return x - jnp.sum(x, axis=0, keepdims=True) * (1.0 / x.shape[0])


def unpack(gathered, first, senders, stride, per, tiles, out):
    for s in range(senders):
        for t in range(tiles):
            out[s * per : (s + 1) * per, t * LANES : (t + 1) * LANES] = gathered[
                pl.ds(s * stride + first + t, per, stride=tiles), :
            ]


def weights_of(now, taper, misfit, variance, zeros, cov, rhs, beside=lambda k: None):
    members, count = now.shape
    tiles = count // LANES
    anom = anomaly(now)
    spread = dot_exact(anom.T, anom) * (1.0 / (members - 1))
    diag = lax.broadcasted_iota(jnp.int32, (count, count), 0) == lax.broadcasted_iota(
        jnp.int32, (count, count), 1
    )
    cov[...] = taper * spread + jnp.where(diag, variance, 0.0)
    rhs[...] = misfit
    corner = cov[0:LANES, 0:LANES]
    for k in range(tiles):
        before = slice(0, k * LANES)
        at = slice(k * LANES, (k + 1) * LANES)
        after = slice((k + 1) * LANES, count)
        inv = inverse_128(corner, zeros)
        if k + 1 < tiles:
            soon = slice((k + 1) * LANES, (k + 2) * LANES)
            low_soon = dot_exact(cov[soon, at], inv)
            corner = cov[soon, soon] - dot_exact(low_soon, cov[at, soon])
            low = low_soon
            if k + 2 < tiles:
                late = slice((k + 2) * LANES, count)
                low_late = dot_exact(cov[late, at], inv)
                cov[soon, late] -= dot_exact(low_soon, cov[at, late])
                cov[late, after] -= dot_exact(low_late, cov[at, after])
                low = jnp.concatenate([low_soon, low_late], axis=0)
        top = dot_exact(rhs[:, at], inv)
        rhs[:, at] = top
        if k + 1 < tiles:
            rhs[:, after] -= dot_exact(top, cov[at, after])
            if k:
                cov[after, before] -= dot_exact(low, cov[at, before])
            cov[after, at] = low
        if k:
            rhs[:, before] -= dot_exact(top, cov[at, before])
        beside(k)
    return anom, rhs[...]


def first_kernel(
    owner, widths, gathered, location, values, noise, variance, zero,
    anom_out, weight_out, pred, cov, rhs, *, senders, extents, lines
):
    members, count = anom_out.shape
    taper = obs_taper(owner, widths, location, 0, 0, extents, lines)
    stride = gathered.shape[0] // senders
    unpack(gathered, 0, senders, stride, members // senders, count // LANES, pred)
    now = pred[...]
    anom_out[...], weight_out[...] = weights_of(
        now, taper, values[0:1, :] + noise[0] - now, variance[0:1, :], zero[...], cov, rhs
    )


def rest_kernel(
    owner, widths, gathered, location, values, noise, variance, zero, anom_first, weight_first, my_row,
    out, anom_all, weight_all, pred, cov, rhs, *, senders, extents, lines, skip, picked_rows
):
    rows_all, cols_all = extents
    blocks, members, count = noise.shape
    per = members // senders
    stride = gathered.shape[0] // senders
    for b in range(1, blocks):
        unpack(
            gathered, skip + (b - 1) * picked_rows, senders, stride, per, count // LANES, pred.at[b]
        )
    unpack(gathered, 0, senders, stride, per, cols_all // LANES, out)
    anom_all[0] = anom_first[...]
    weight_all[0] = weight_first[...]
    row = my_row[0].astype(f32)
    share = 1.0 / (members - 1)

    def own_variables(b):
        obs_row, obs_col = obs_place(owner[b], location[pl.ds(b, 1), :], cols_all, lines)
        inv_row, inv_col = inverse_of(widths[b, 0]), inverse_of(widths[b, 1])
        left = stacked(anom_all[b]).T.astype(bf16)
        by_row = across(obs_row, lambda x: ring_taper(row, x, float(rows_all), inv_row))
        weight = weight_all[b] * (by_row * share)
        obs_col = down(obs_col, count)

        def part(k, parts=count // LANES):
            size = cols_all // parts
            at = slice(k * size, (k + 1) * size)
            now = out[:, at]
            cross = dot_stacked(left, anomaly(now))
            lane = lax.broadcasted_iota(jnp.int32, (1, size), 1).astype(f32) + float(k * size)
            by_col = across(lane, lambda x: ring_taper(obs_col, x, float(cols_all), inv_col))
            out[:, at] = now + dot_split(weight, by_col * cross)

        return part

    def predict(a, c):
        now = pred[c]
        left = stacked(anom_all[a]).T.astype(bf16)
        cross = dot_stacked(left, anomaly(now)) * share
        taper = obs_taper(owner, widths, location, a, c, extents, lines)
        pred[c] = now + dot_split(weight_all[a], taper * cross)

    for b in range(1, blocks):
        predict(b - 1, b)
        now = pred[b]
        part = own_variables(b - 1)

        def beside(k, b=b, part=part):
            part(k)
            if k == 0:
                for c in range(b + 1, blocks):
                    predict(b - 1, c)

        anom_all[b], weight_all[b] = weights_of(
            now,
            obs_taper(owner, widths, location, b, b, extents, lines),
            values[b : b + 1, :] + noise[b] - now,
            variance[b : b + 1, :],
            zero[...],
            cov,
            rhs,
            beside,
        )
    own_variables(blocks - 1)(0, 1)


def solve(kernel, args, outs, scratch, count, members, **sizes):
    def body(*refs):
        kernel(*refs, **sizes)

    return pl.pallas_call(
        body,
        out_shape=[jax.ShapeDtypeStruct(shape, f32) for shape in outs],
        in_specs=[smem] * 2 + [vmem] * 8 + [smem] if len(args) == 11 else [smem] * 2 + [vmem] * 6,
        out_specs=[vmem] * len(outs),
        scratch_shapes=[pltpu.VMEM(shape, f32) for shape in scratch]
        + [pltpu.VMEM((count, count), f32), pltpu.VMEM((members, count), f32)],
        compiler_params=params,
        name="solve",
    )(*args)


def choose_kernel(owner, received, state, first, second, *, used):
    receivers = first.shape[0]
    own_rows = state.shape[0] // receivers
    blocks = owner.shape[0]
    chunk = [received[owner[b]] for b in range(blocks)]
    for m in range(receivers):
        first[m] = chunk[0]
        second[m, 0:own_rows, :] = state[m * own_rows : (m + 1) * own_rows, :]
        for b in range(1, blocks):
            at = own_rows + (b - 1) * used
            second[m, at : at + used, :] = chunk[b][:used]


def choose(owner, received, state, receivers, used):
    rows = received.shape[1]
    blocks = owner.shape[0]
    own_rows = state.shape[0] // receivers

    def body(*refs):
        choose_kernel(*refs, used=used)

    return pl.pallas_call(
        body,
        out_shape=[
            jax.ShapeDtypeStruct((receivers, rows, LANES), f32),
            jax.ShapeDtypeStruct((receivers, own_rows + (blocks - 1) * used, LANES), f32),
        ],
        in_specs=[smem, vmem, vmem],
        out_specs=[vmem, vmem],
        compiler_params=params,
        name="choose",
    )(owner, received, state)


def shards(
    starting_sample_set, block_owner, obs_location, taper_pairs, obs_values, obs_noise, obs_variance
):
    members, fields, lines, width = starting_sample_set.shape
    regions = lax.axis_size("reg")
    senders = lax.axis_size("mem")
    region = lax.axis_index("reg")
    mem_index = lax.axis_index("mem")
    extents = (lines * regions, width)
    assert fields * lines == senders

    forth = [(i, (i + 1) % regions) for i in range(regions)]
    back = [((i + 1) % regions, i) for i in range(regions)]
    above = lax.ppermute(starting_sample_set, "reg", forth)
    below = lax.ppermute(starting_sample_set, "reg", back)

    loc, own = prepare(block_owner, region.reshape(1), obs_location, starting_sample_set)
    state, picked = forecast(above, own, below, loc, regions)

    picked_rows = picked.shape[0] // regions
    picked = lax.all_to_all(
        picked.reshape(regions, picked_rows, LANES), "reg", 0, 0, tiled=True
    )
    skip = members * GROUP
    used = members * obs_location.shape[1] // LANES
    first, second = choose(block_owner, picked, state, senders, used)
    first = lax.all_to_all(first, "mem", 0, 0, tiled=True)
    first, second = lax.optimization_barrier((first, second))
    second = lax.all_to_all(second, "mem", 0, 0, tiled=True).reshape(-1, LANES)

    zero = jnp.zeros((GROUP, LANES), f32)
    my_row = (region * lines + mem_index % lines).reshape(1)
    one = obs_noise.shape[1:]
    sizes = dict(count=one[1], members=one[0], senders=senders, extents=extents, lines=lines)
    common = (obs_location, obs_values, obs_noise, obs_variance, zero)
    done = solve(
        first_kernel,
        (block_owner, taper_pairs, first.reshape(-1, LANES)) + common,
        (one, one),
        (one,),
        **sizes,
    )
    return solve(
        rest_kernel,
        (block_owner, taper_pairs, second) + common + tuple(done) + (my_row,),
        ((one[0], width),),
        (obs_noise.shape,) * 3,
        skip=skip,
        picked_rows=used,
        **sizes,
    )[0]


def solution(mesh):
    return jax.shard_map(
        shards,
        mesh=mesh,
        in_specs=(P("mem", None, "reg", None), P(), P(), P(), P(), P(), P()),
        out_specs=P(None, ("reg", "mem")),
        check_vma=False,
    )
```
